32 devices in a mesh: row: 8 (over y, x, core), col: 4 (over z).
Axes of the slice: x: 2, y: 2, z: 4, core: 2. Of those that a mesh axis runs over, the one named last changes fastest.
Arguments:
- pair_feature_map: bfloat16 [64, 512, 512], P(None, 'row', 'col'), may hold values from -6 to 6
- conv_weight: bfloat16 [3, 3, 64, 64], replicated, may hold values from -0.25 to 0.25
- conv_bias: float32 [64], replicated, may hold values from -3 to 3
- cotangent: bfloat16 [64, 512, 512], P(None, 'row', 'col'), may hold values from -6 to 6
Outputs:
- symmetric: bfloat16 [64, 512, 512], P(None, 'row', 'col')
- grad_input: bfloat16 [64, 512, 512], P(None, 'row', 'col')
- grad_weight: float32 [3, 3, 64, 64], replicated
- grad_bias: float32 [64], replicated
The draws below stay inside these ranges and needn't reach their ends.
All inputs are finite; a program needn't handle non-finite values.
Results may differ from the reference program's by a relative error of at most 0.0085.
Values may be sent and summed in bfloat16 or wider, within the bound.
No kernel may reach another device: no remote copies, remote signals or barrier semaphores. Data moves between devices by JAX's collectives and lax.ppermute only.
A program may use at most 128 MiB of HBM per device.

```python
import jax
import jax.numpy as jnp
from jax import lax

C = 64
DILATION_STEP = 8
L = 512


def steps_of(stream_key, extent, cuts, low, high):
    factor_of, own = 1.0, jax.random.fold_in(stream_key, 6)
    for dim, blocks in cuts:
        draws = jnp.exp(jax.random.uniform(jax.random.fold_in(own, dim), (blocks,), jnp.float32, low / len(cuts), high / len(cuts)))
        factor_of = factor_of * jnp.repeat(draws, extent[dim] // blocks).reshape([-1 if axis == dim else 1 for axis in range(len(extent))])
    return factor_of


def centred(rng, shape, spread, limit, split=(), dtype=jnp.bfloat16):
    values = jax.random.normal(rng, shape, jnp.float32) * spread
    if len(split) > 0:
        values = steps_of(rng, shape, split, -0.22, 0.18) * values
    return jnp.clip(values, min=-limit, max=limit).astype(dtype)


def setup_inputs(seed: int = 0) -> dict:
    streams_of = jax.random.split(jax.random.key(seed), 5)
    return {
        "pair_feature_map": centred(streams_of[0], (C, L, L), 1.0, 6.0, ((1, 8), (2, 4))),
        "conv_weight": centred(streams_of[1], (3, 3, C, C), (9 * C) ** -0.5, 0.25),
        "conv_bias": centred(streams_of[2], (C,), 0.5, 3.0, (), jnp.float32),
        "cotangent": centred(streams_of[3], (C, L, L), 1.0, 6.0, ((1, 8), (2, 4))),
    }


def tap_block(padded_input, conv_weight, leading_row, block_row_span, flip):
    channel_count = padded_input.shape[0]
    map_width = padded_input.shape[2] - 2 * DILATION_STEP
    anchor_point = jnp.zeros((), jnp.int32)
    total = jnp.zeros((channel_count, block_row_span, map_width), jnp.float32)
    for row_kernel_tap in range(3):
        for column_tap in range(3):
            row_offset = 2 - row_kernel_tap if flip else row_kernel_tap
            column_offset = 2 - column_tap if flip else column_tap
            block_portion = lax.dynamic_slice(padded_input, (anchor_point, leading_row + DILATION_STEP * row_offset, anchor_point + DILATION_STEP * column_offset), (channel_count, block_row_span, map_width)).astype(jnp.float32)
            matrix = conv_weight[row_kernel_tap, column_tap].astype(jnp.float32)
            if flip:
                matrix = matrix.T
            total = total + jnp.einsum("oi,ihw->ohw", matrix, block_portion)
    return total


def weight_block(gradient_padded, pair_feature_map, leading_row, block_row_span):
    channel_count = pair_feature_map.shape[0]
    map_width = pair_feature_map.shape[2]
    anchor_point = jnp.zeros((), jnp.int32)
    rows_x = lax.dynamic_slice(pair_feature_map, (anchor_point, leading_row, anchor_point), (channel_count, block_row_span, map_width)).astype(jnp.float32)
    grads = []
    for row_kernel_tap in range(3):
        for column_tap in range(3):
            block_portion = lax.dynamic_slice(gradient_padded, (anchor_point, leading_row + DILATION_STEP * (2 - row_kernel_tap), anchor_point + DILATION_STEP * (2 - column_tap)), (channel_count, block_row_span, map_width)).astype(jnp.float32)
            grads.append(jnp.einsum("ohw,ihw->oi", block_portion, rows_x))
    return jnp.stack(grads).reshape(3, 3, channel_count, channel_count)


def join_blocks(stacked):
    return jnp.transpose(stacked, (1, 0, 2, 3)).reshape(stacked.shape[1], -1, stacked.shape[3])


def reference(pair_feature_map, conv_weight, conv_bias, cotangent):
    block_count = 8
    block_row_span = L // block_count
    starts = (jnp.arange(block_count) * block_row_span).astype(jnp.int32)
    border_edges = ((0, 0), (DILATION_STEP, DILATION_STEP), (DILATION_STEP, DILATION_STEP))
    padded_input = jnp.pad(pair_feature_map, border_edges)
    pre_blocks = lax.map(lambda leading_row: tap_block(padded_input, conv_weight, leading_row, block_row_span, False), starts)
    pre_act = join_blocks(pre_blocks) + conv_bias[:, None, None]
    mixed_map = (pair_feature_map.astype(jnp.float32) + jax.nn.elu(pre_act)).astype(jnp.bfloat16)
    symmetric = (mixed_map.astype(jnp.float32) + jnp.transpose(mixed_map, (0, 2, 1)).astype(jnp.float32)).astype(jnp.bfloat16)
    grad_mixed = cotangent.astype(jnp.float32) + jnp.transpose(cotangent, (0, 2, 1)).astype(jnp.float32)
    elu_slope = jnp.where(pre_act > 0, jnp.float32(1.0), jnp.exp(jnp.minimum(pre_act, jnp.float32(0.0))))
    gradient_preactivation = (grad_mixed * elu_slope).astype(jnp.bfloat16)
    gradient_padded = jnp.pad(gradient_preactivation, border_edges)

    def backward(leading_row):
        back = tap_block(gradient_padded, conv_weight, leading_row, block_row_span, True)
        return back, weight_block(gradient_padded, pair_feature_map, leading_row, block_row_span)

    back_blocks, weight_parts = lax.map(backward, starts)
    grad_input = (grad_mixed + join_blocks(back_blocks)).astype(jnp.bfloat16)
    grad_weight = jnp.sum(weight_parts, axis=0) / L
    grad_bias = jnp.sum(gradient_preactivation.astype(jnp.float32), axis=(1, 2)) / L
    return symmetric, grad_input, grad_weight, grad_bias
```

```python
import functools

import jax
import jax.numpy as jnp
from jax import lax
from jax.experimental import pallas as pl
from jax.experimental.pallas import tpu as pltpu
from jax.sharding import PartitionSpec as P

DILATION_STEP = 8
STEP = DILATION_STEP
BF16, F32 = jnp.bfloat16, jnp.float32
VMEM_LIMIT = 40 * 1024 * 1024


def call(kernel, out_shape, *args, scratch=(), flops=0, name=None):
    out_bytes = sum(o.size * o.dtype.itemsize for o in jax.tree.leaves(out_shape))
    in_bytes = sum(a.size * a.dtype.itemsize for a in args)
    return pl.pallas_call(
        kernel,
        out_shape=out_shape,
        scratch_shapes=scratch,
        name=name,
        compiler_params=pltpu.CompilerParams(vmem_limit_bytes=VMEM_LIMIT),
        cost_estimate=pl.CostEstimate(
            flops=flops, bytes_accessed=in_bytes + out_bytes, transcendentals=0
        ),
    )(*args)


def shape(dims, dtype):
    return jax.ShapeDtypeStruct(tuple(dims), dtype)


def columns_of(rows, first):
    picked = [r[:, :STEP] if first else r[:, -STEP:] for r in rows]
    return jnp.concatenate(picked, axis=1)


def write_edges(tile, up_ref, down_ref, left_ref, right_ref):
    tile_rows, _, tile_cols = tile.shape
    span = tile_cols // STEP
    for group in range(tile_rows // span):
        rows = [tile[group * span + k] for k in range(span)]
        left_ref[group] = columns_of(rows, True)
        right_ref[group] = columns_of(rows, False)
    top = [tile[k] for k in range(STEP)]
    bottom = [tile[tile_rows - STEP + k] for k in range(STEP)]
    for k in range(STEP):
        up_ref[k] = bottom[k]
        down_ref[k] = top[k]
    up_ref[STEP] = jnp.concatenate([columns_of(bottom, True), columns_of(bottom, False)], axis=1)
    down_ref[STEP] = jnp.concatenate([columns_of(top, False), columns_of(top, True)], axis=1)


def edge_shapes(channels, tile_rows, tile_cols):
    message = shape((STEP + 1, channels, tile_cols), BF16)
    strips = shape((tile_rows * STEP // tile_cols, channels, tile_cols), BF16)
    return [message, message, strips, strips]


def exchange_edges(up, down, left, right):
    half = up.shape[2] // 2
    rows, cols = lax.axis_size("row"), lax.axis_size("col")
    up_row = [(i, i + 1) for i in range(rows - 1)]
    up_col = [(i, i + 1) for i in range(cols - 1)]
    before = lax.ppermute(up, "row", up_row)
    after = lax.ppermute(down, "row", [(j, i) for i, j in up_row])
    lower = lax.broadcasted_iota(jnp.int32, (1, 1, up.shape[2]), 2) < half
    corner_left = jnp.where(lower, before[STEP:], after[STEP:])
    corner_right = jnp.where(lower, after[STEP:], before[STEP:])
    from_right = lax.ppermute(
        jnp.concatenate([left, corner_left]), "col", [(j, i) for i, j in up_col]
    )
    from_left = lax.ppermute(jnp.concatenate([right, corner_right]), "col", up_col)
    return before, after, from_left, from_right


def write_shifted(tile, before, after, from_left, from_right, stack):
    tile_rows, channels, tile_cols = tile.shape
    span = tile_cols // STEP
    corner = tile_rows // span
    half = tile_cols // 2
    for row in range(tile_rows + 2 * STEP):
        own = row - STEP
        if own < 0:
            middle, group, at_left, at_right = before[row], corner, half + STEP * row, STEP * row
        elif own >= tile_rows:
            k = own - tile_rows
            middle, group, at_left, at_right = after[k], corner, STEP * k, half + STEP * k
        else:
            middle, group = tile[own], own // span
            at_left = at_right = STEP * (own % span)
        left = from_left[group][:, at_left : at_left + STEP]
        right = from_right[group][:, at_right : at_right + STEP]
        stack[row, :channels] = jnp.concatenate([left, middle[:, :-STEP]], axis=1)
        stack[row, channels : 2 * channels] = middle
        stack[row, 2 * channels :] = jnp.concatenate([middle[:, STEP:], right], axis=1)


def convolve(stack, matrix, tile_rows, emit):
    channels = matrix.shape[0] // 3
    cols = stack.shape[2]
    weights = matrix[...]
    for pair in range(STEP // 2):
        products = []
        for k in range(tile_rows // STEP + 2):
            row = STEP * k + 2 * pair
            both = jnp.concatenate([stack[row], stack[row + 1]], axis=1)
            products.append(jnp.dot(weights, both, preferred_element_type=F32))
            if k >= 2:
                total = (
                    products[k - 2][:channels]
                    + products[k - 1][channels : 2 * channels]
                    + products[k][2 * channels :]
                )
                out_row = STEP * (k - 2) + 2 * pair
                emit(out_row, total[:, :cols])
                emit(out_row + 1, total[:, cols:])


def split_kernel(x, tile, up, down, left, right):
    rows = x.shape[1]
    for a in range(0, rows, 16):
        tile[a : a + 16] = jnp.swapaxes(x[:, a : a + 16], 0, 1)
    write_edges(tile, up, down, left, right)


def forward_kernel(
    tile, before, after, from_left, from_right, matrix, bias, stack, mixed, slope, kept
):
    tile_rows = tile.shape[0]
    write_shifted(tile, before, after, from_left, from_right, stack)
    offset = bias[...]

    def emit(row, total):
        pre_act = total + offset
        rise = jnp.exp(jnp.minimum(pre_act, 0.0))
        slope[row] = rise
        elu = jnp.where(pre_act > 0, pre_act, rise - 1.0)
        kept[row] = (tile[row].astype(F32) + elu).astype(BF16)

    convolve(stack, matrix, tile_rows, emit)
    for a in range(0, tile_rows, 16):
        mixed[:, a : a + 16] = jnp.swapaxes(kept[a : a + 16], 0, 1)


def grad_pre_kernel(cot, mirrored, slope, tile, up, down, left, right):
    rows = cot.shape[1]
    for a in range(0, rows, 16):
        grad_mixed = cot[:, a : a + 16].astype(F32) + mirrored[:, a : a + 16].astype(F32)
        tile[a : a + 16] = (jnp.swapaxes(grad_mixed, 0, 1) * slope[a : a + 16]).astype(BF16)
    write_edges(tile, up, down, left, right)


def weight_kernel(side, grad, stack, packed):
    tile_rows, channels, cols = grad.shape
    nothing = jnp.zeros((channels, cols), BF16)

    def taps(row):
        own = [row - STEP * p for p in range(3)]
        return jnp.concatenate([grad[a] if 0 <= a < tile_rows else nothing for a in own], axis=0)

    total = jnp.zeros((3 * channels, 3 * channels), F32)
    for row in range(0, tile_rows + 2 * STEP, 2):
        total = total + lax.dot_general(
            jnp.concatenate([taps(row), taps(row + 1)], axis=1),
            jnp.concatenate([stack[row], stack[row + 1]], axis=1),
            (((1,), (1,)), ((), ())),
            preferred_element_type=F32,
        )
    cells = jnp.zeros((channels, cols), F32)
    for row in range(tile_rows):
        cells = cells + grad[row].astype(F32)
    bias = jnp.broadcast_to(jnp.sum(cells, axis=1, keepdims=True), (channels, channels))
    blocks = [
        total[p * channels : (p + 1) * channels, q * channels : (q + 1) * channels]
        for p in range(3)
        for q in range(3)
    ] + [bias]
    for k in range(0, len(blocks), 2):
        packed[k // 2] = jnp.concatenate(blocks[k : k + 2], axis=1) * (1.0 / side)


def unpack_kernel(mine, other, weight, bias):
    channels = mine.shape[1]
    for k in range(9):
        at = channels * (k % 2)
        block = mine[k // 2] + other[k // 2]
        weight[k // 3, k % 3] = block[:, at : at + channels]
    last = mine[4][:, channels:] + other[4][:, channels:]
    line = lax.broadcasted_iota(jnp.int32, last.shape, 0)
    lane = lax.broadcasted_iota(jnp.int32, last.shape, 1)
    bias[...] = jnp.sum(jnp.where(line == lane, last, 0.0), axis=0, keepdims=True)


def input_grad_kernel(
    tile, before, after, from_left, from_right, matrix, cot, mirrored, out, stack, kept
):
    tile_rows = tile.shape[0]
    write_shifted(tile, before, after, from_left, from_right, stack)

    def emit(row, total):
        kept[row] = total

    convolve(stack, matrix, tile_rows, emit)
    for a in range(0, tile_rows, 16):
        grad_mixed = cot[:, a : a + 16].astype(F32) + mirrored[:, a : a + 16].astype(F32)
        out[:, a : a + 16] = (grad_mixed + jnp.swapaxes(kept[a : a + 16], 0, 1)).astype(BF16)


def turn_kernel(add, *refs):
    if add:
        source, own, out = refs
    else:
        source, out = refs
    cols_of, ratio, channels, tile_rows, tile_cols = source.shape
    for z in range(cols_of):
        for c in range(channels):
            square = jnp.concatenate([source[z, e, c] for e in range(ratio)], axis=0)
            turned = square.T
            for h in range(ratio):
                part = turned[h * tile_rows : (h + 1) * tile_rows]
                if add:
                    part = (part.astype(F32) + own[z, h, c].astype(F32)).astype(BF16)
                out[z, h, c] = part


def mirror(x, add):
    channels, tile_rows, tile_cols = x.shape
    rows, cols = lax.axis_size("row"), lax.axis_size("col")
    ratio = tile_cols // tile_rows
    blocks = (cols, ratio, channels // rows, tile_rows, tile_cols)
    dealt = lax.all_to_all(x, "row", split_axis=0, concat_axis=0, tiled=True)
    moved = lax.all_to_all(dealt, "col", split_axis=0, concat_axis=0, tiled=True)
    args = [moved.reshape(blocks)] + ([dealt.reshape(blocks)] if add else [])
    turned = call(
        functools.partial(turn_kernel, add),
        shape(blocks, BF16),
        *args,
        name="turn_and_add" if add else "turn",
    )
    return lax.all_to_all(turned.reshape(x.shape), "row", split_axis=0, concat_axis=0, tiled=True)


def summed(part):
    hops = []
    for axis in ("row", "col"):
        size, reach = lax.axis_size(axis), 1
        while reach < size:
            hops.append((axis, [(i, i ^ reach) for i in range(size)]))
            reach *= 2
    for axis, pairs in hops[:-1]:
        part = part + lax.ppermute(part, axis, pairs)
    axis, pairs = hops[-1]
    return part, lax.ppermute(part, axis, pairs)


def shards(pair_feature_map, conv_weight, conv_bias, cotangent):
    channels, tile_rows, tile_cols = pair_feature_map.shape
    side = tile_rows * lax.axis_size("row")
    tile_shape = shape((tile_rows, channels, tile_cols), BF16)
    edges = edge_shapes(channels, tile_rows, tile_cols)
    stack_dims = (tile_rows + 2 * STEP, 3 * channels, tile_cols)
    conv_flops = 2 * 9 * channels * channels * tile_rows * tile_cols
    w_front = jnp.transpose(conv_weight, (0, 2, 1, 3)).reshape(3 * channels, 3 * channels)
    w_back = jnp.transpose(conv_weight[::-1, ::-1], (0, 3, 1, 2)).reshape(
        3 * channels, 3 * channels
    )

    mirrored = mirror(cotangent, False)

    tile, *edge = call(split_kernel, [tile_shape] + edges, pair_feature_map, name="split")
    halo = exchange_edges(*edge)
    stack, mixed, slope = call(
        forward_kernel,
        [
            shape(stack_dims, BF16),
            shape(pair_feature_map.shape, BF16),
            shape((tile_rows, channels, tile_cols), F32),
        ],
        tile,
        *halo,
        w_front,
        conv_bias[:, None],
        scratch=[pltpu.VMEM((tile_rows, channels, tile_cols), BF16)],
        flops=conv_flops,
        name="forward",
    )
    symmetric = mirror(mixed, True)

    grad, *edge = call(
        grad_pre_kernel, [tile_shape] + edges, cotangent, mirrored, slope, name="grad_pre"
    )
    packed = call(
        functools.partial(weight_kernel, side),
        shape((5, channels, 2 * channels), F32),
        grad,
        stack,
        flops=conv_flops,
        name="weight_terms",
    )
    halo = exchange_edges(*edge)
    grad_input = call(
        input_grad_kernel,
        shape(pair_feature_map.shape, BF16),
        grad,
        *halo,
        w_back,
        cotangent,
        mirrored,
        scratch=[
            pltpu.VMEM(stack_dims, BF16),
            pltpu.VMEM((tile_rows, channels, tile_cols), F32),
        ],
        flops=conv_flops,
        name="input_grad",
    )
    grad_weight, grad_bias = call(
        unpack_kernel,
        [shape((3, 3, channels, channels), F32), shape((1, channels), F32)],
        *summed(packed),
        name="unpack",
    )
    return symmetric, grad_input, grad_weight, grad_bias.reshape(channels)


def solution(mesh):
    placed = (P(None, "row", "col"), P(), P(), P(None, "row", "col"))
    return jax.shard_map(
        shards,
        mesh=mesh,
        in_specs=placed,
        out_specs=(P(None, "row", "col"), P(None, "row", "col"), P(), P()),
        check_vma=False,
    )
```

```python
import functools

import jax
import jax.numpy as jnp
from jax import lax
from jax.experimental import pallas as pl
from jax.experimental.pallas import tpu as pltpu
from jax.sharding import PartitionSpec as P

DILATION_STEP = 8
STEP = DILATION_STEP
BF16, F32 = jnp.bfloat16, jnp.float32
VMEM_LIMIT = 40 * 1024 * 1024


def call(kernel, out_shape, *args, scratch=(), flops=0, name=None):
    out_bytes = sum(o.size * o.dtype.itemsize for o in jax.tree.leaves(out_shape))
    in_bytes = sum(a.size * a.dtype.itemsize for a in args)
    in_specs = [
        pl.BlockSpec(memory_space=pltpu.SMEM if a.dtype == jnp.int32 else pltpu.VMEM) for a in args
    ]
    return pl.pallas_call(
        kernel,
        out_shape=out_shape,
        in_specs=in_specs,
        scratch_shapes=scratch,
        name=name,
        compiler_params=pltpu.CompilerParams(vmem_limit_bytes=VMEM_LIMIT),
        cost_estimate=pl.CostEstimate(
            flops=flops, bytes_accessed=in_bytes + out_bytes, transcendentals=0
        ),
    )(*args)


def shape(dims, dtype):
    return jax.ShapeDtypeStruct(tuple(dims), dtype)


def columns_of(rows, first):
    picked = [r[:, :STEP] if first else r[:, -STEP:] for r in rows]
    return jnp.concatenate(picked, axis=1)


def write_edges(tile, up_ref, down_ref, left_ref, right_ref):
    tile_rows, _, tile_cols = tile.shape
    span = tile_cols // STEP
    for group in range(tile_rows // span):
        rows = [tile[group * span + k] for k in range(span)]
        left_ref[group] = columns_of(rows, True)
        right_ref[group] = columns_of(rows, False)
    top = [tile[k] for k in range(STEP)]
    bottom = [tile[tile_rows - STEP + k] for k in range(STEP)]
    for k in range(STEP):
        up_ref[k] = bottom[k]
        down_ref[k] = top[k]
    up_ref[STEP] = jnp.concatenate([columns_of(bottom, True), columns_of(bottom, False)], axis=1)
    down_ref[STEP] = jnp.concatenate([columns_of(top, False), columns_of(top, True)], axis=1)


def edge_shapes(channels, tile_rows, tile_cols):
    message = shape((STEP + 1, channels, tile_cols), BF16)
    strips = shape((tile_rows * STEP // tile_cols, channels, tile_cols), BF16)
    return [message, message, strips, strips]


def exchange_edges(up, down, left, right):
    half = up.shape[2] // 2
    rows, cols = lax.axis_size("row"), lax.axis_size("col")
    up_row = [(i, i + 1) for i in range(rows - 1)]
    up_col = [(i, i + 1) for i in range(cols - 1)]
    before = lax.ppermute(up, "row", up_row)
    after = lax.ppermute(down, "row", [(j, i) for i, j in up_row])
    lower = lax.broadcasted_iota(jnp.int32, (1, 1, up.shape[2]), 2) < half
    corner_left = jnp.where(lower, before[STEP:], after[STEP:])
    corner_right = jnp.where(lower, after[STEP:], before[STEP:])
    from_right = lax.ppermute(
        jnp.concatenate([left, corner_left]), "col", [(j, i) for i, j in up_col]
    )
    from_left = lax.ppermute(jnp.concatenate([right, corner_right]), "col", up_col)
    return before, after, from_left, from_right


def write_shifted(tile, before, after, from_left, from_right, stack):
    tile_rows, channels, tile_cols = tile.shape
    span = tile_cols // STEP
    corner = tile_rows // span
    half = tile_cols // 2
    for row in range(tile_rows + 2 * STEP):
        own = row - STEP
        if own < 0:
            middle, group, at_left, at_right = before[row], corner, half + STEP * row, STEP * row
        elif own >= tile_rows:
            k = own - tile_rows
            middle, group, at_left, at_right = after[k], corner, STEP * k, half + STEP * k
        else:
            middle, group = tile[own], own // span
            at_left = at_right = STEP * (own % span)
        left = from_left[group][:, at_left : at_left + STEP]
        right = from_right[group][:, at_right : at_right + STEP]
        stack[row, :channels] = jnp.concatenate([left, middle[:, :-STEP]], axis=1)
        stack[row, channels : 2 * channels] = middle
        stack[row, 2 * channels :] = jnp.concatenate([middle[:, STEP:], right], axis=1)


def forward_taps(weight):
    lines = [jnp.concatenate([weight[p, q] for q in range(3)], axis=1) for p in range(3)]
    return jnp.concatenate(lines, axis=0)


def backward_taps(weight):
    lines = [
        jnp.concatenate([weight[2 - p, 2 - q].T for q in range(3)], axis=1) for p in range(3)
    ]
    return jnp.concatenate(lines, axis=0)


def convolve(stack, weights, tile_rows, emit):
    channels = weights.shape[0] // 3
    cols = stack.shape[2]
    for pair in range(STEP // 2):
        products = []
        for k in range(tile_rows // STEP + 2):
            row = STEP * k + 2 * pair
            both = jnp.concatenate([stack[row], stack[row + 1]], axis=1)
            products.append(jnp.dot(weights, both, preferred_element_type=F32))
            if k >= 2:
                total = (
                    products[k - 2][:channels]
                    + products[k - 1][channels : 2 * channels]
                    + products[k][2 * channels :]
                )
                out_row = STEP * (k - 2) + 2 * pair
                emit(out_row, total[:, :cols])
                emit(out_row + 1, total[:, cols:])


def split_kernel(x, tile, up, down, left, right):
    rows = x.shape[1]
    for a in range(0, rows, 16):
        tile[a : a + 16] = jnp.swapaxes(x[:, a : a + 16], 0, 1)
    write_edges(tile, up, down, left, right)


def forward_kernel(
    place, tile, before, after, from_left, from_right, weight, bias, stack, mixed, slope, *rest
):
    pieces, kept = rest[:-1], rest[-1]
    tile_rows = tile.shape[0]
    write_shifted(tile, before, after, from_left, from_right, stack)
    offset = bias[...]

    def emit(row, total):
        pre_act = total + offset
        rise = jnp.exp(jnp.minimum(pre_act, 0.0))
        slope[row] = rise
        elu = jnp.where(pre_act > 0, pre_act, rise - 1.0)
        kept[row] = (tile[row].astype(F32) + elu).astype(BF16)

    convolve(stack, forward_taps(weight), tile_rows, emit)
    for a in range(0, tile_rows, 16):
        mixed[:, a : a + 16] = jnp.swapaxes(kept[a : a + 16], 0, 1)
    deal_kernel(place, mixed, *pieces)


def grad_pre_kernel(
    groups, place, cot, keep, got, slope, tile, up, down, left, right, mirrored
):
    rows = cot.shape[1]
    for a in range(0, rows, 16):
        turned = joined(place[1], keep[:, a : a + 16], got[:, a : a + 16], groups)
        mirrored[:, a : a + 16] = turned.astype(BF16)
        grad_mixed = cot[:, a : a + 16].astype(F32) + turned
        tile[a : a + 16] = (jnp.swapaxes(grad_mixed, 0, 1) * slope[a : a + 16]).astype(BF16)
    write_edges(tile, up, down, left, right)


def weight_kernel(side, grad, stack, packed):
    tile_rows, channels, cols = grad.shape
    nothing = jnp.zeros((channels, cols), BF16)

    def taps(row):
        own = [row - STEP * p for p in range(3)]
        return jnp.concatenate([grad[a] if 0 <= a < tile_rows else nothing for a in own], axis=0)

    total = jnp.zeros((3 * channels, 3 * channels), F32)
    for row in range(0, tile_rows + 2 * STEP, 2):
        total = total + lax.dot_general(
            jnp.concatenate([taps(row), taps(row + 1)], axis=1),
            jnp.concatenate([stack[row], stack[row + 1]], axis=1),
            (((1,), (1,)), ((), ())),
            preferred_element_type=F32,
        )
    cells = jnp.zeros((channels, cols), F32)
    for row in range(tile_rows):
        cells = cells + grad[row].astype(F32)
    bias = jnp.broadcast_to(jnp.sum(cells, axis=1, keepdims=True), (channels, channels))
    blocks = [
        total[p * channels : (p + 1) * channels, q * channels : (q + 1) * channels]
        for p in range(3)
        for q in range(3)
    ] + [bias]
    for k in range(0, len(blocks), 2):
        packed[k // 2] = jnp.concatenate(blocks[k : k + 2], axis=1) * (1.0 / side)


def unpack_kernel(mine, other, weight, bias):
    channels = mine.shape[1]
    for k in range(9):
        at = channels * (k % 2)
        block = mine[k // 2] + other[k // 2]
        weight[k // 3, k % 3] = block[:, at : at + channels]
    last = mine[4][:, channels:] + other[4][:, channels:]
    line = lax.broadcasted_iota(jnp.int32, last.shape, 0)
    lane = lax.broadcasted_iota(jnp.int32, last.shape, 1)
    bias[...] = jnp.sum(jnp.where(line == lane, last, 0.0), axis=0, keepdims=True)


def input_grad_kernel(
    tile, before, after, from_left, from_right, weight, cot, mirrored, out, stack, kept
):
    tile_rows = tile.shape[0]
    write_shifted(tile, before, after, from_left, from_right, stack)

    def emit(row, total):
        kept[row] = total

    convolve(stack, backward_taps(weight), tile_rows, emit)
    for a in range(0, tile_rows, 16):
        grad_mixed = cot[:, a : a + 16].astype(F32) + mirrored[:, a : a + 16].astype(F32)
        out[:, a : a + 16] = (grad_mixed + jnp.swapaxes(kept[a : a + 16], 0, 1)).astype(BF16)


def deal_kernel(place, x, *pieces):
    group = x.shape[0] // len(pieces)
    for j, piece in enumerate(pieces):
        piece[...] = x[pl.ds((place[0] ^ j) * group, group)]


def turn_kernel(place, *refs):
    pieces, (keep, give) = refs[:-2], refs[-2:]
    group, tile_rows, tile_cols = pieces[0].shape
    half = group // 2
    core = place[1]
    for j, piece in enumerate(pieces):
        at = (place[2] ^ j) * half
        for c in range(half):
            low, high = piece[c].T, piece[c + half].T
            first = jnp.concatenate([low[:tile_rows], high[:tile_rows]], axis=1)
            second = jnp.concatenate([low[tile_rows:], high[tile_rows:]], axis=1)
            keep[at + c] = jnp.where(core == 0, first, second)
            give[at + c] = jnp.where(core == 0, second, first)


def joined(core, keep, got, groups):
    keep, got = keep.astype(F32), got.astype(F32)
    pairs, rows, cols = keep.shape
    lower = lax.broadcasted_iota(jnp.int32, (1, 1, cols), 2) < cols // 2
    first, second = jnp.where(core == 0, keep, got), jnp.where(core == 0, got, keep)
    low = jnp.where(lower, first, swap_lanes(second))
    high = jnp.where(lower, swap_lanes(first), second)
    shaped = [v.reshape(groups, pairs // groups, rows, cols) for v in (low, high)]
    return jnp.concatenate(shaped, axis=1).reshape(2 * pairs, rows, cols)


def swap_lanes(x):
    half = x.shape[2] // 2
    return jnp.concatenate([x[:, :, half:], x[:, :, :half]], axis=2)


def places():
    row = lax.axis_index("row")
    return jnp.stack([row // 2, row % 2, lax.axis_index("col")]).astype(jnp.int32)


def dealt(x, place):
    rounds = lax.axis_size("col")
    piece = shape((x.shape[0] // rounds,) + x.shape[1:], x.dtype)
    return call(deal_kernel, [piece] * rounds, place, x, name="deal")


def mirror(pieces, place):
    rounds, size = lax.axis_size("col"), lax.axis_size("row")
    arrived = []
    for j, piece in enumerate(pieces):
        if j:
            piece = lax.ppermute(piece, "row", [(r, r ^ (2 * j)) for r in range(size)])
        owners = [
            (r * rounds + z, (z * 2 + r % 2) * rounds + ((r // 2) ^ j))
            for r in range(size)
            for z in range(rounds)
        ]
        arrived.append(lax.ppermute(piece, ("row", "col"), owners))
    group, tile_rows, tile_cols = pieces[0].shape
    half = shape((group * rounds // 2, tile_rows, tile_cols), BF16)
    keep, give = call(turn_kernel, [half, half], place, *arrived, name="turn")
    got = lax.ppermute(give, "row", [(r, r ^ 1) for r in range(size)])
    return keep, got


def join_kernel(groups, place, own, keep, got, out):
    for a in range(0, own.shape[1], 16):
        rows = slice(a, a + 16)
        turned = joined(place[1], keep[:, rows], got[:, rows], groups)
        out[:, rows] = (own[:, rows].astype(F32) + turned).astype(BF16)


def summed(part):
    hops = []
    for axis in ("row", "col"):
        size, reach = lax.axis_size(axis), 1
        while reach < size:
            hops.append((axis, [(i, i ^ reach) for i in range(size)]))
            reach *= 2
    for axis, pairs in hops[:-1]:
        part = part + lax.ppermute(part, axis, pairs)
    axis, pairs = hops[-1]
    return part, lax.ppermute(part, axis, pairs)


def shards(pair_feature_map, conv_weight, conv_bias, cotangent):
    channels, tile_rows, tile_cols = pair_feature_map.shape
    side = tile_rows * lax.axis_size("row")
    tile_shape = shape((tile_rows, channels, tile_cols), BF16)
    edges = edge_shapes(channels, tile_rows, tile_cols)
    stack_dims = (tile_rows + 2 * STEP, 3 * channels, tile_cols)
    conv_flops = 2 * 9 * channels * channels * tile_rows * tile_cols
    rounds = lax.axis_size("col")
    place = places()

    keep, got = mirror(dealt(cotangent, place), place)

    tile, *edge = call(split_kernel, [tile_shape] + edges, pair_feature_map, name="split")
    halo = exchange_edges(*edge)
    piece = shape((channels // rounds, tile_rows, tile_cols), BF16)
    stack, mixed, slope, *pieces = call(
        forward_kernel,
        [
            shape(stack_dims, BF16),
            shape(pair_feature_map.shape, BF16),
            shape((tile_rows, channels, tile_cols), F32),
        ]
        + [piece] * rounds,
        place,
        tile,
        *halo,
        conv_weight,
        conv_bias[:, None],
        scratch=[pltpu.VMEM((tile_rows, channels, tile_cols), BF16)],
        flops=conv_flops,
        name="forward",
    )
    mixed_keep, mixed_got = mirror(pieces, place)
    symmetric = call(
        functools.partial(join_kernel, rounds),
        shape(mixed.shape, BF16),
        place,
        mixed,
        mixed_keep,
        mixed_got,
        name="join",
    )

    grad, *edge, mirrored = call(
        functools.partial(grad_pre_kernel, rounds),
        [tile_shape] + edges + [shape(cotangent.shape, BF16)],
        place,
        cotangent,
        keep,
        got,
        slope,
        name="grad_pre",
    )
    packed = call(
        functools.partial(weight_kernel, side),
        shape((5, channels, 2 * channels), F32),
        grad,
        stack,
        flops=conv_flops,
        name="weight_terms",
    )
    halo = exchange_edges(*edge)
    grad_input = call(
        input_grad_kernel,
        shape(pair_feature_map.shape, BF16),
        grad,
        *halo,
        conv_weight,
        cotangent,
        mirrored,
        scratch=[
            pltpu.VMEM(stack_dims, BF16),
            pltpu.VMEM((tile_rows, channels, tile_cols), F32),
        ],
        flops=conv_flops,
        name="input_grad",
    )
    grad_weight, grad_bias = call(
        unpack_kernel,
        [shape((3, 3, channels, channels), F32), shape((1, channels), F32)],
        *summed(packed),
        name="unpack",
    )
    return symmetric, grad_input, grad_weight, grad_bias.reshape(channels)


def solution(mesh):
    placed = (P(None, "row", "col"), P(), P(), P(None, "row", "col"))
    return jax.shard_map(
        shards,
        mesh=mesh,
        in_specs=placed,
        out_specs=(P(None, "row", "col"), P(None, "row", "col"), P(), P()),
        check_vma=False,
    )
```

```python
import functools

import jax
import jax.numpy as jnp
from jax import lax
from jax.experimental import pallas as pl
from jax.experimental.pallas import tpu as pltpu
from jax.sharding import PartitionSpec as P

DILATION_STEP = 8
STEP = DILATION_STEP
BF16, F32 = jnp.bfloat16, jnp.float32
VMEM_LIMIT = 24 * 1024 * 1024


def call(kernel, out_shape, *args, scratch=(), flops=0, in_hbm=(), out_hbm=0, name=None):
    out_bytes = sum(o.size * o.dtype.itemsize for o in jax.tree.leaves(out_shape))
    in_bytes = sum(a.size * a.dtype.itemsize for a in args)
    in_specs = [
        pl.BlockSpec(memory_space=pltpu.SMEM if a.dtype == jnp.int32 else pltpu.VMEM) for a in args
    ]
    for k in in_hbm:
        in_specs[k] = pl.BlockSpec(memory_space=pl.ANY)
    out_specs = [pl.BlockSpec(memory_space=pltpu.VMEM)] * len(jax.tree.leaves(out_shape))
    if out_hbm:
        out_specs[-out_hbm:] = [pl.BlockSpec(memory_space=pl.ANY)] * out_hbm
    if not isinstance(out_shape, list):
        out_specs = out_specs[0]
    return pl.pallas_call(
        kernel,
        out_shape=out_shape,
        in_specs=in_specs,
        out_specs=out_specs,
        scratch_shapes=scratch,
        name=name,
        compiler_params=pltpu.CompilerParams(vmem_limit_bytes=VMEM_LIMIT),
        cost_estimate=pl.CostEstimate(
            flops=flops, bytes_accessed=in_bytes + out_bytes, transcendentals=0
        ),
    )(*args)


def shape(dims, dtype):
    return jax.ShapeDtypeStruct(tuple(dims), dtype)


def columns_of(rows, first):
    picked = [r[:, :STEP] if first else r[:, -STEP:] for r in rows]
    return jnp.concatenate(picked, axis=1)


def write_edges(tile, top_ref, bottom_ref, left_ref, right_ref):
    tile_rows, _, tile_cols = tile.shape
    span = tile_cols // STEP
    for group in range(tile_rows // span):
        rows = [tile[group * span + k] for k in range(span)]
        left_ref[group] = columns_of(rows, True)
        right_ref[group] = columns_of(rows, False)
    for k in range(STEP):
        top_ref[k] = tile[k]
        bottom_ref[k] = tile[tile_rows - STEP + k]


def edge_shapes(channels, tile_rows, tile_cols):
    rows = shape((STEP, channels, tile_cols), BF16)
    strips = shape((tile_rows * STEP // tile_cols, channels, tile_cols), BF16)
    return [rows, rows, strips, strips]


def shift(x, axis, forward):
    pairs = [(i, i + 1) for i in range(lax.axis_size(axis) - 1)]
    return lax.ppermute(x, axis, pairs if forward else [(j, i) for i, j in pairs])


def columns_first(top, bottom, left, right):
    from_left, from_right = shift(right, "col", True), shift(left, "col", False)
    last = left.shape[0] - 1
    down = jnp.concatenate([top, from_left[:1], from_right[:1]])
    up = jnp.concatenate([bottom, from_left[last:], from_right[last:]])
    return shift(up, "row", True), shift(down, "row", False), from_left, from_right


def corner_kernel(before, after, left, right, left_out, right_out):
    groups = left.shape[0]
    rows = [edge[k] for edge in (before, after) for k in range(STEP)]
    for first, strips, out in ((True, left, left_out), (False, right, right_out)):
        out[:groups] = strips[...]
        out[groups] = columns_of(rows, first)


def rows_first(top, bottom, left, right):
    before, after = shift(bottom, "row", True), shift(top, "row", False)
    whole = shape((left.shape[0] + 1,) + left.shape[1:], BF16)
    left, right = call(
        corner_kernel, [whole, whole], before, after, left, right, name="corners"
    )
    from_right, from_left = shift(left, "col", False), shift(right, "col", True)
    return before, after, from_left, from_right


def write_shifted(tile, before, after, from_left, from_right, stack):
    tile_rows, channels, tile_cols = tile.shape
    span = tile_cols // STEP
    groups = tile_rows // span
    rows_carry_corners = before.shape[0] > STEP
    for row in range(tile_rows + 2 * STEP):
        own = row - STEP
        if 0 <= own < tile_rows:
            middle, lane = tile[own], STEP * (own % span)
            left, right = from_left[own // span], from_right[own // span]
        else:
            edge, k = (before, row) if own < 0 else (after, own - tile_rows)
            middle = edge[k]
            if rows_carry_corners:
                left, right = edge[STEP], edge[STEP + 1]
                lane = STEP * (k + span - STEP if own < 0 else k)
            else:
                left, right = from_left[groups], from_right[groups]
                lane = STEP * (k if own < 0 else k + STEP)
        left, right = left[:, lane : lane + STEP], right[:, lane : lane + STEP]
        stack[row, :channels] = jnp.concatenate([left, middle[:, :-STEP]], axis=1)
        stack[row, channels : 2 * channels] = middle
        stack[row, 2 * channels :] = jnp.concatenate([middle[:, STEP:], right], axis=1)


def forward_taps(weight):
    lines = [jnp.concatenate([weight[p, q] for q in range(3)], axis=1) for p in range(3)]
    return jnp.concatenate(lines, axis=0)


def backward_taps(weight):
    lines = [
        jnp.concatenate([weight[2 - p, 2 - q].T for q in range(3)], axis=1) for p in range(3)
    ]
    return jnp.concatenate(lines, axis=0)


def convolve(stack, weights, tile_rows, emit):
    channels = weights.shape[0] // 3
    cols = stack.shape[2]
    for pair in range(STEP // 2):
        products = []
        for k in range(tile_rows // STEP + 2):
            row = STEP * k + 2 * pair
            both = jnp.concatenate([stack[row], stack[row + 1]], axis=1)
            products.append(jnp.dot(weights, both, preferred_element_type=F32))
            if k >= 2:
                total = (
                    products[k - 2][:channels]
                    + products[k - 1][channels : 2 * channels]
                    + products[k][2 * channels :]
                )
                out_row = STEP * (k - 2) + 2 * pair
                emit(out_row, total[:, :cols])
                emit(out_row + 1, total[:, cols:])


def open_kernel(cot, x, tile, top, bottom, left, right, *rest):
    pieces, done = rest[:-1], rest[-1]
    group = pieces[0].shape[0]
    copies = [
        pltpu.make_async_copy(cot.at[pl.ds(j * group, group)], piece, done.at[j])
        for j, piece in enumerate(pieces)
    ]
    for copy in copies:
        copy.start()
    rows = x.shape[1]
    for a in range(0, rows, 16):
        tile[a : a + 16] = jnp.swapaxes(x[:, a : a + 16], 0, 1)
    write_edges(tile, top, bottom, left, right)
    for copy in copies:
        copy.wait()


def forward_kernel(
    tile, before, after, from_left, from_right, weight, bias, token, stack, slope, *refs
):
    pieces, kept = refs[:-1], refs[-1]
    token[...] = jnp.zeros_like(token)
    group = pieces[0].shape[0]
    tile_rows = tile.shape[0]
    write_shifted(tile, before, after, from_left, from_right, stack)
    offset = bias[...]

    def emit(row, total):
        pre_act = total + offset
        rise = jnp.exp(jnp.minimum(pre_act, 0.0))
        slope[row] = rise
        elu = jnp.where(pre_act > 0, pre_act, rise - 1.0)
        kept[row] = (tile[row].astype(F32) + elu).astype(BF16)

    convolve(stack, forward_taps(weight), tile_rows, emit)
    for a in range(0, tile_rows, 16):
        mixed = jnp.swapaxes(kept[a : a + 16], 0, 1)
        for j, piece in enumerate(pieces):
            piece[:, a : a + 16] = mixed[j * group : (j + 1) * group]


def grad_pre_kernel(place, cot, keep, got, slope, token, tile, top, bottom, left, right, mirrored):
    token[...] = jnp.zeros_like(token)
    rows = cot.shape[1]
    for a in range(0, rows, 16):
        turned = joined(place[0], keep[:, a : a + 16], got[:, a : a + 16])
        mirrored[:, a : a + 16] = turned.astype(BF16)
        grad_mixed = cot[:, a : a + 16].astype(F32) + turned
        tile[a : a + 16] = (jnp.swapaxes(grad_mixed, 0, 1) * slope[a : a + 16]).astype(BF16)
    write_edges(tile, top, bottom, left, right)


def weight_kernel(side, place, grad, stack, token, keep, give, packed):
    token[...] = jnp.zeros_like(token)
    tile_rows, channels, cols = grad.shape
    nothing = jnp.zeros((channels, cols), BF16)

    def taps(row):
        own = [row - STEP * p for p in range(3)]
        return jnp.concatenate([grad[a] if 0 <= a < tile_rows else nothing for a in own], axis=0)

    total = jnp.zeros((3 * channels, 3 * channels), F32)
    for row in range(0, tile_rows + 2 * STEP, 2):
        total = total + lax.dot_general(
            jnp.concatenate([taps(row), taps(row + 1)], axis=1),
            jnp.concatenate([stack[row], stack[row + 1]], axis=1),
            (((1,), (1,)), ((), ())),
            preferred_element_type=F32,
        )
    cells = jnp.zeros((channels, cols), F32)
    for row in range(tile_rows):
        cells = cells + grad[row].astype(F32)
    bias = jnp.broadcast_to(jnp.sum(cells, axis=1, keepdims=True), (channels, channels))
    blocks = [
        total[p * channels : (p + 1) * channels, q * channels : (q + 1) * channels]
        for p in range(3)
        for q in range(3)
    ] + [bias]
    for k in range(0, len(blocks), 2):
        at = k // 2 * channels
        packed[at : at + channels] = jnp.concatenate(blocks[k : k + 2], axis=1) * (1.0 / side)
    half = keep.shape[0]
    keep[...] = packed[pl.ds(place[0] * half, half)]
    give[...] = packed[pl.ds((1 - place[0]) * half, half)]


def unpack_kernel(place, mine, other, weight, bias, packed):
    half, channels = mine.shape[0], weight.shape[2]
    packed[pl.ds(place[0] * half, half)] = mine[...]
    packed[pl.ds((1 - place[0]) * half, half)] = other[...]
    for k in range(9):
        row, col = k // 2 * channels, k % 2 * channels
        weight[k // 3, k % 3] = packed[row : row + channels, col : col + channels]
    last = packed[4 * channels :, channels:]
    line = lax.broadcasted_iota(jnp.int32, last.shape, 0)
    lane = lax.broadcasted_iota(jnp.int32, last.shape, 1)
    bias[...] = jnp.sum(jnp.where(line == lane, last, 0.0), axis=0, keepdims=True)


def input_grad_kernel(
    tile, before, after, from_left, from_right, weight, cot, mirrored, out, stack, kept
):
    tile_rows = tile.shape[0]
    write_shifted(tile, before, after, from_left, from_right, stack)

    def emit(row, total):
        kept[row] = total

    convolve(stack, backward_taps(weight), tile_rows, emit)
    for a in range(0, tile_rows, 16):
        grad_mixed = cot[:, a : a + 16].astype(F32) + mirrored[:, a : a + 16].astype(F32)
        out[:, a : a + 16] = (grad_mixed + jnp.swapaxes(kept[a : a + 16], 0, 1)).astype(BF16)


def turn_kernel(place, *refs):
    pieces, (keep, give) = refs[:-2], refs[-2:]
    tile_rows = pieces[0].shape[1]
    core = place[0]
    group, near = pieces[0].shape[0], len(pieces) // 2
    for j in range(near):
        for c in range(group):
            low, high = pieces[j][c].T, pieces[j + near][c].T
            first = jnp.concatenate([low[:tile_rows], high[:tile_rows]], axis=1)
            second = jnp.concatenate([low[tile_rows:], high[tile_rows:]], axis=1)
            keep[j * group + c] = jnp.where(core == 0, first, second)
            give[j * group + c] = jnp.where(core == 0, second, first)


def joined(core, keep, got):
    keep, got = keep.astype(F32), got.astype(F32)
    lower = lax.broadcasted_iota(jnp.int32, (1, 1, keep.shape[2]), 2) < keep.shape[2] // 2
    first, second = jnp.where(core == 0, keep, got), jnp.where(core == 0, got, keep)
    low = jnp.where(lower, first, swap_lanes(second))
    high = jnp.where(lower, swap_lanes(first), second)
    return jnp.concatenate([low, high], axis=0)


def swap_lanes(x):
    half = x.shape[2] // 2
    return jnp.concatenate([x[:, :, half:], x[:, :, :half]], axis=2)


def detour(piece, far):
    if far == 0:
        return piece
    return lax.ppermute(piece, "row", [(r, r ^ (2 * far)) for r in range(lax.axis_size("row"))])


def cross(piece, far):
    size, blocks = lax.axis_size("row"), lax.axis_size("col")
    owners = [
        (r * blocks + z, (z * 2 + r % 2) * blocks + ((r // 2) ^ far))
        for r in range(size)
        for z in range(blocks)
    ]
    return lax.ppermute(piece, ("row", "col"), owners)


def turn(pieces, place):
    group, tile_rows, tile_cols = pieces[0].shape
    half = shape((group * len(pieces) // 2, tile_rows, tile_cols), BF16)
    return call(turn_kernel, [half, half], place, *pieces, name="turn")


def swapped(give):
    return lax.ppermute(give, "row", [(r, r ^ 1) for r in range(lax.axis_size("row"))])


def held(pieces, *until):
    return lax.optimization_barrier((pieces, until))[0]


def join_kernel(place, keep, got, *refs):
    pieces, out = refs[:-1], refs[-1]
    for a in range(0, out.shape[1], 16):
        rows = slice(a, a + 16)
        turned = joined(place[0], keep[:, rows], got[:, rows])
        own = jnp.concatenate([piece[:, rows] for piece in pieces], axis=0)
        out[:, rows] = (own.astype(F32) + turned).astype(BF16)


def summed(part, axis, reach):
    size = lax.axis_size(axis)
    while reach < size:
        part = part + lax.ppermute(part, axis, [(i, i ^ reach) for i in range(size)])
        reach *= 2
    return part


def shards(pair_feature_map, conv_weight, conv_bias, cotangent):
    channels, tile_rows, tile_cols = pair_feature_map.shape
    side = tile_rows * lax.axis_size("row")
    tile_shape = shape((tile_rows, channels, tile_cols), BF16)
    edges = edge_shapes(channels, tile_rows, tile_cols)
    stack_dims = (tile_rows + 2 * STEP, 3 * channels, tile_cols)
    conv_flops = 2 * 9 * channels * channels * tile_rows * tile_cols
    rounds = lax.axis_size("col")
    place = jnp.full((1,), lax.axis_index("row") % 2, jnp.int32)
    piece = shape((channels // rounds, tile_rows, tile_cols), BF16)

    tile, *opened = call(
        open_kernel,
        [tile_shape] + edges + [piece] * rounds,
        cotangent,
        pair_feature_map,
        scratch=[pltpu.SemaphoreType.DMA((rounds,))],
        in_hbm=[0],
        out_hbm=rounds,
        name="open",
    )
    token = shape((8, 128), F32)
    halo = columns_first(*opened[:4])
    dealt = [detour(p, j) for j, p in enumerate(opened[4:])]
    forwarded, stack, slope, *mixed = call(
        forward_kernel,
        [token, shape(stack_dims, BF16), shape((tile_rows, channels, tile_cols), F32)]
        + [piece] * rounds,
        tile,
        *halo,
        conv_weight,
        conv_bias[:, None],
        scratch=[pltpu.VMEM((tile_rows, channels, tile_cols), BF16)],
        flops=conv_flops,
        name="forward",
    )
    arrived = [cross(held(p, *halo[2:]), j) for j, p in enumerate(dealt)]
    mixed_dealt = [detour(p, j) for j, p in enumerate(mixed)]
    keep, give = turn(held(arrived, slope), place)
    ready, grad, *edge, mirrored = call(
        grad_pre_kernel,
        [token, tile_shape] + edges + [shape(cotangent.shape, BF16)],
        place,
        cotangent,
        keep,
        swapped(give),
        slope,
        name="grad_pre",
    )
    packed = pltpu.VMEM((5 * channels, 2 * channels), F32)
    half = shape((5 * channels // 2, 2 * channels), F32)
    weighed, *terms = call(
        functools.partial(weight_kernel, side),
        [token, half, half],
        place,
        grad,
        stack,
        scratch=[packed],
        flops=conv_flops,
        name="weight_terms",
    )
    halo = columns_first(*edge)
    part = summed(terms[0] + swapped(terms[1]), "col", 1)
    mixed_arrived = [cross(held(p, part, *halo[2:]), j) for j, p in enumerate(mixed_dealt)]
    part = summed(part, "row", 2)
    mixed_keep, mixed_give = turn(held(mixed_arrived, part, *halo[:2]), place)
    symmetric = call(
        join_kernel,
        shape(pair_feature_map.shape, BF16),
        place,
        mixed_keep,
        swapped(mixed_give),
        *mixed,
        name="join",
    )
    grad_input = call(
        input_grad_kernel,
        shape(pair_feature_map.shape, BF16),
        grad,
        *halo,
        conv_weight,
        cotangent,
        mirrored,
        scratch=[
            pltpu.VMEM(stack_dims, BF16),
            pltpu.VMEM((tile_rows, channels, tile_cols), F32),
        ],
        flops=conv_flops,
        name="input_grad",
    )
    grad_weight, grad_bias = call(
        unpack_kernel,
        [shape((3, 3, channels, channels), F32), shape((1, channels), F32)],
        place,
        part,
        swapped(part),
        scratch=[packed],
        name="unpack",
    )
    return symmetric, grad_input, grad_weight, grad_bias.reshape(channels)


def solution(mesh):
    placed = (P(None, "row", "col"), P(), P(), P(None, "row", "col"))
    return jax.shard_map(
        shards,
        mesh=mesh,
        in_specs=placed,
        out_specs=(P(None, "row", "col"), P(None, "row", "col"), P(), P()),
        check_vma=False,
    )
```

```python
import functools

import jax
import jax.numpy as jnp
from jax import lax
from jax.experimental import pallas as pl
from jax.experimental.pallas import tpu as pltpu
from jax.sharding import PartitionSpec as P

DILATION_STEP = 8
STEP = DILATION_STEP
BF16, F32 = jnp.bfloat16, jnp.float32
VMEM_LIMIT = 24 * 1024 * 1024


def call(kernel, out_shape, *args, scratch=(), flops=0, in_hbm=(), out_hbm=0, name=None):
    out_bytes = sum(o.size * o.dtype.itemsize for o in jax.tree.leaves(out_shape))
    in_bytes = sum(a.size * a.dtype.itemsize for a in args)
    in_specs = [
        pl.BlockSpec(memory_space=pltpu.SMEM if a.dtype == jnp.int32 else pltpu.VMEM) for a in args
    ]
    for k in in_hbm:
        in_specs[k] = pl.BlockSpec(memory_space=pl.ANY)
    out_specs = [pl.BlockSpec(memory_space=pltpu.VMEM)] * len(jax.tree.leaves(out_shape))
    if out_hbm:
        out_specs[-out_hbm:] = [pl.BlockSpec(memory_space=pl.ANY)] * out_hbm
    if not isinstance(out_shape, list):
        out_specs = out_specs[0]
    return pl.pallas_call(
        kernel,
        out_shape=out_shape,
        in_specs=in_specs,
        out_specs=out_specs,
        scratch_shapes=scratch,
        name=name,
        compiler_params=pltpu.CompilerParams(vmem_limit_bytes=VMEM_LIMIT),
        cost_estimate=pl.CostEstimate(
            flops=flops, bytes_accessed=in_bytes + out_bytes, transcendentals=0
        ),
    )(*args)


def shape(dims, dtype):
    return jax.ShapeDtypeStruct(tuple(dims), dtype)


def columns_of(rows, first):
    picked = [r[:, :STEP] if first else r[:, -STEP:] for r in rows]
    return jnp.concatenate(picked, axis=1)


def write_pair(parity, start, end, first, second):
    first[...] = jnp.where(parity == 0, end, start)
    second[...] = jnp.where(parity == 0, start, end)


def picked(parity, first, second):
    return jnp.where(parity == 0, second, first), jnp.where(parity == 0, first, second)


def write_edges(row_odd, col_odd, tile, top_ref, bottom_ref, first_ref, second_ref):
    tile_rows, _, tile_cols = tile.shape
    span = tile_cols // STEP
    for group in range(tile_rows // span):
        rows = [tile[group * span + k] for k in range(span)]
        write_pair(
            col_odd[0],
            columns_of(rows, True),
            columns_of(rows, False),
            first_ref.at[group],
            second_ref.at[group],
        )
    for k in range(STEP):
        top_ref[k] = tile[k]
        bottom_ref[k] = tile[tile_rows - STEP + k]


def edge_shapes(channels, tile_rows, tile_cols):
    rows = shape((STEP, channels, tile_cols), BF16)
    strips = shape((tile_rows * STEP // tile_cols, channels, tile_cols), BF16)
    return [rows, rows, strips, strips]


def exchanged(first, second, axis):
    size = lax.axis_size(axis)
    pairs = [[(i, i + 1) for i in range(k, size - 1, 2)] for k in range(2)]
    return [
        lax.ppermute(x, axis, pair + [(j, i) for i, j in pair])
        for x, pair in zip((first, second), pairs)
    ]


def message_kernel(row_odd, col_odd, top, bottom, first, second, row_first, row_second):
    last = first.shape[0] - 1
    write_pair(row_odd[0], top[...], bottom[...], row_first.at[:STEP], row_second.at[:STEP])
    starts = picked(col_odd[0], first[0], second[0])
    ends = picked(col_odd[0], first[last], second[last])
    for k in range(2):
        write_pair(
            row_odd[0], starts[k], ends[k], row_first.at[STEP + k], row_second.at[STEP + k]
        )


def halo_of(place, top, bottom, first, second):
    strips = exchanged(first, second, "col")
    message = shape((STEP + 2,) + top.shape[1:], BF16)
    rows = call(
        message_kernel, [message, message], *place, top, bottom, *strips, name="messages"
    )
    return *exchanged(*rows, "row"), *strips


def write_shifted(row_odd, col_odd, tile, row_first, row_second, col_first, col_second, stack):
    tile_rows, channels, tile_cols = tile.shape
    span = tile_cols // STEP
    before, after = picked(row_odd[0], row_first[...], row_second[...])
    from_left, from_right = picked(col_odd[0], col_first[...], col_second[...])
    for row in range(tile_rows + 2 * STEP):
        own = row - STEP
        if 0 <= own < tile_rows:
            middle, lane = tile[own], STEP * (own % span)
            left, right = from_left[own // span], from_right[own // span]
        else:
            edge, k = (before, row) if own < 0 else (after, own - tile_rows)
            middle, left, right = edge[k], edge[STEP], edge[STEP + 1]
            lane = STEP * (k + span - STEP if own < 0 else k)
        left, right = left[:, lane : lane + STEP], right[:, lane : lane + STEP]
        stack[row, :channels] = jnp.concatenate([left, middle[:, :-STEP]], axis=1)
        stack[row, channels : 2 * channels] = middle
        stack[row, 2 * channels :] = jnp.concatenate([middle[:, STEP:], right], axis=1)


def forward_taps(weight):
    lines = [jnp.concatenate([weight[p, q] for q in range(3)], axis=1) for p in range(3)]
    return jnp.concatenate(lines, axis=0)


def backward_taps(weight):
    lines = [
        jnp.concatenate([weight[2 - p, 2 - q].T for q in range(3)], axis=1) for p in range(3)
    ]
    return jnp.concatenate(lines, axis=0)


def convolve(stack, weights, tile_rows, emit):
    channels = weights.shape[0] // 3
    cols = stack.shape[2]
    for pair in range(STEP // 2):
        products = []
        for k in range(tile_rows // STEP + 2):
            row = STEP * k + 2 * pair
            both = jnp.concatenate([stack[row], stack[row + 1]], axis=1)
            products.append(jnp.dot(weights, both, preferred_element_type=F32))
            if k >= 2:
                total = (
                    products[k - 2][:channels]
                    + products[k - 1][channels : 2 * channels]
                    + products[k][2 * channels :]
                )
                out_row = STEP * (k - 2) + 2 * pair
                emit(out_row, total[:, :cols])
                emit(out_row + 1, total[:, cols:])


def open_kernel(row_odd, col_odd, cot, x, tile, top, bottom, first, second, *rest):
    pieces, done = rest[:-1], rest[-1]
    group = pieces[0].shape[0]
    copies = [
        pltpu.make_async_copy(cot.at[pl.ds(j * group, group)], piece, done.at[j])
        for j, piece in enumerate(pieces)
    ]
    for copy in copies:
        copy.start()
    rows = x.shape[1]
    for a in range(0, rows, 16):
        tile[a : a + 16] = jnp.swapaxes(x[:, a : a + 16], 0, 1)
    write_edges(row_odd, col_odd, tile, top, bottom, first, second)
    for copy in copies:
        copy.wait()


def forward_kernel(row_odd, col_odd, tile, *refs):
    halo, (weight, bias, token, stack, slope, *pieces, kept) = refs[:4], refs[4:]
    token[...] = jnp.zeros_like(token)
    group = pieces[0].shape[0]
    tile_rows = tile.shape[0]
    write_shifted(row_odd, col_odd, tile, *halo, stack)
    offset = bias[...]

    def emit(row, total):
        pre_act = total + offset
        rise = jnp.exp(jnp.minimum(pre_act, 0.0))
        slope[row] = rise
        elu = jnp.where(pre_act > 0, pre_act, rise - 1.0)
        kept[row] = (tile[row].astype(F32) + elu).astype(BF16)

    convolve(stack, forward_taps(weight), tile_rows, emit)
    for a in range(0, tile_rows, 16):
        mixed = jnp.swapaxes(kept[a : a + 16], 0, 1)
        for j, piece in enumerate(pieces):
            piece[:, a : a + 16] = mixed[j * group : (j + 1) * group]


def grad_pre_kernel(
    row_odd, col_odd, cot, keep, got, slope, token, tile, top, bottom, first, second, mirrored
):
    token[...] = jnp.zeros_like(token)
    rows = cot.shape[1]
    for a in range(0, rows, 16):
        turned = joined(row_odd[0], keep[:, a : a + 16], got[:, a : a + 16])
        mirrored[:, a : a + 16] = turned.astype(BF16)
        grad_mixed = cot[:, a : a + 16].astype(F32) + turned
        tile[a : a + 16] = (jnp.swapaxes(grad_mixed, 0, 1) * slope[a : a + 16]).astype(BF16)
    write_edges(row_odd, col_odd, tile, top, bottom, first, second)


def weight_kernel(side, row_odd, grad, stack, token, keep, give, packed):
    token[...] = jnp.zeros_like(token)
    tile_rows, channels, cols = grad.shape
    nothing = jnp.zeros((channels, cols), BF16)

    def taps(row):
        own = [row - STEP * p for p in range(3)]
        return jnp.concatenate([grad[a] if 0 <= a < tile_rows else nothing for a in own], axis=0)

    total = jnp.zeros((3 * channels, 3 * channels), F32)
    for row in range(0, tile_rows + 2 * STEP, 2):
        total = total + lax.dot_general(
            jnp.concatenate([taps(row), taps(row + 1)], axis=1),
            jnp.concatenate([stack[row], stack[row + 1]], axis=1),
            (((1,), (1,)), ((), ())),
            preferred_element_type=F32,
        )
    cells = jnp.zeros((channels, cols), F32)
    for row in range(tile_rows):
        cells = cells + grad[row].astype(F32)
    bias = jnp.broadcast_to(jnp.sum(cells, axis=1, keepdims=True), (channels, channels))
    blocks = [
        total[p * channels : (p + 1) * channels, q * channels : (q + 1) * channels]
        for p in range(3)
        for q in range(3)
    ] + [bias]
    for k in range(0, len(blocks), 2):
        at = k // 2 * channels
        packed[at : at + channels] = jnp.concatenate(blocks[k : k + 2], axis=1) * (1.0 / side)
    half = keep.shape[0]
    keep[...] = packed[pl.ds(row_odd[0] * half, half)]
    give[...] = packed[pl.ds((1 - row_odd[0]) * half, half)]


def unpack_kernel(row_odd, mine, other, weight, bias, packed):
    half, channels = mine.shape[0], weight.shape[2]
    packed[pl.ds(row_odd[0] * half, half)] = mine[...]
    packed[pl.ds((1 - row_odd[0]) * half, half)] = other[...]
    for k in range(9):
        row, col = k // 2 * channels, k % 2 * channels
        weight[k // 3, k % 3] = packed[row : row + channels, col : col + channels]
    last = packed[4 * channels :, channels:]
    line = lax.broadcasted_iota(jnp.int32, last.shape, 0)
    lane = lax.broadcasted_iota(jnp.int32, last.shape, 1)
    bias[...] = jnp.sum(jnp.where(line == lane, last, 0.0), axis=0, keepdims=True)


def input_grad_kernel(row_odd, col_odd, tile, *refs):
    halo, (weight, cot, mirrored, token, out, stack, kept) = refs[:4], refs[4:]
    token[...] = jnp.zeros_like(token)
    tile_rows = tile.shape[0]
    write_shifted(row_odd, col_odd, tile, *halo, stack)

    def emit(row, total):
        kept[row] = total

    convolve(stack, backward_taps(weight), tile_rows, emit)
    for a in range(0, tile_rows, 16):
        grad_mixed = cot[:, a : a + 16].astype(F32) + mirrored[:, a : a + 16].astype(F32)
        out[:, a : a + 16] = (grad_mixed + jnp.swapaxes(kept[a : a + 16], 0, 1)).astype(BF16)


def turn_kernel(unread, row_odd, *refs):
    pieces, (keep, give) = refs[unread:-2], refs[-2:]
    tile_rows = pieces[0].shape[1]
    core = row_odd[0]
    group, near = pieces[0].shape[0], len(pieces) // 2
    for j in range(near):
        for c in range(group):
            low, high = pieces[j][c].T, pieces[j + near][c].T
            first = jnp.concatenate([low[:tile_rows], high[:tile_rows]], axis=1)
            second = jnp.concatenate([low[tile_rows:], high[tile_rows:]], axis=1)
            keep[j * group + c] = jnp.where(core == 0, first, second)
            give[j * group + c] = jnp.where(core == 0, second, first)


def joined(core, keep, got):
    keep, got = keep.astype(F32), got.astype(F32)
    lower = lax.broadcasted_iota(jnp.int32, (1, 1, keep.shape[2]), 2) < keep.shape[2] // 2
    first, second = jnp.where(core == 0, keep, got), jnp.where(core == 0, got, keep)
    low = jnp.where(lower, first, swap_lanes(second))
    high = jnp.where(lower, swap_lanes(first), second)
    return jnp.concatenate([low, high], axis=0)


def swap_lanes(x):
    half = x.shape[2] // 2
    return jnp.concatenate([x[:, :, half:], x[:, :, :half]], axis=2)


def detour(piece, far):
    if far == 0:
        return piece
    return lax.ppermute(piece, "row", [(r, r ^ (2 * far)) for r in range(lax.axis_size("row"))])


def cross(piece, far):
    size, blocks = lax.axis_size("row"), lax.axis_size("col")
    owners = [
        (r * blocks + z, (z * 2 + r % 2) * blocks + ((r // 2) ^ far))
        for r in range(size)
        for z in range(blocks)
    ]
    return lax.ppermute(piece, ("row", "col"), owners)


def turn(pieces, place, *after):
    group, tile_rows, tile_cols = pieces[0].shape
    half = shape((group * len(pieces) // 2, tile_rows, tile_cols), BF16)
    kernel = functools.partial(turn_kernel, len(after))
    return call(kernel, [half, half], place[0], *after, *pieces, name="turn")


def swapped(give):
    return lax.ppermute(give, "row", [(r, r ^ 1) for r in range(lax.axis_size("row"))])


def held(pieces, *until):
    return lax.optimization_barrier((pieces, until))[0]


def join_kernel(row_odd, keep, got, *refs):
    pieces, out = refs[:-1], refs[-1]
    for a in range(0, out.shape[1], 16):
        rows = slice(a, a + 16)
        turned = joined(row_odd[0], keep[:, rows], got[:, rows])
        own = jnp.concatenate([piece[:, rows] for piece in pieces], axis=0)
        out[:, rows] = (own.astype(F32) + turned).astype(BF16)


def summed(part, axis, reach):
    size = lax.axis_size(axis)
    while reach < size:
        part = part + lax.ppermute(part, axis, [(i, i ^ reach) for i in range(size)])
        reach *= 2
    return part


def shards(pair_feature_map, conv_weight, conv_bias, cotangent):
    channels, tile_rows, tile_cols = pair_feature_map.shape
    side = tile_rows * lax.axis_size("row")
    tile_shape = shape((tile_rows, channels, tile_cols), BF16)
    edges = edge_shapes(channels, tile_rows, tile_cols)
    stack_dims = (tile_rows + 2 * STEP, 3 * channels, tile_cols)
    conv_flops = 2 * 9 * channels * channels * tile_rows * tile_cols
    rounds = lax.axis_size("col")
    place = [jnp.full((1,), lax.axis_index(axis) % 2, jnp.int32) for axis in ("row", "col")]
    piece = shape((channels // rounds, tile_rows, tile_cols), BF16)

    tile, *opened = call(
        open_kernel,
        [tile_shape] + edges + [piece] * rounds,
        *place,
        cotangent,
        pair_feature_map,
        scratch=[pltpu.SemaphoreType.DMA((rounds,))],
        in_hbm=[2],
        out_hbm=rounds,
        name="open",
    )
    token = shape((8, 128), F32)
    dealt = [detour(p, j) for j, p in enumerate(opened[4:])]
    halo = halo_of(place, *opened[:4])
    forwarded, stack, slope, *mixed = call(
        forward_kernel,
        [token, shape(stack_dims, BF16), shape((tile_rows, channels, tile_cols), F32)]
        + [piece] * rounds,
        *place,
        tile,
        *halo,
        conv_weight,
        conv_bias[:, None],
        scratch=[pltpu.VMEM((tile_rows, channels, tile_cols), BF16)],
        flops=conv_flops,
        name="forward",
    )
    arrived = [cross(held(p, *halo[2:]), j) for j, p in enumerate(dealt)]
    mixed_dealt = [detour(p, j) for j, p in enumerate(mixed)]
    keep, give = turn(held(arrived, slope), place)
    ready, grad, *edge, mirrored = call(
        grad_pre_kernel,
        [token, tile_shape] + edges + [shape(cotangent.shape, BF16)],
        *place,
        cotangent,
        keep,
        swapped(give),
        slope,
        name="grad_pre",
    )
    packed = pltpu.VMEM((5 * channels, 2 * channels), F32)
    half = shape((5 * channels // 2, 2 * channels), F32)
    weighed, *terms = call(
        functools.partial(weight_kernel, side),
        [token, half, half],
        place[0],
        grad,
        stack,
        scratch=[packed],
        flops=conv_flops,
        name="weight_terms",
    )
    part = summed(terms[0] + swapped(terms[1]), "col", 1)
    across = summed(part, "row", 2)
    halo = halo_of(place, *edge)
    mixed_arrived = [cross(held(p, part), j) for j, p in enumerate(mixed_dealt)]
    ended, grad_input = call(
        input_grad_kernel,
        [token, shape(pair_feature_map.shape, BF16)],
        *place,
        grad,
        *halo,
        conv_weight,
        cotangent,
        mirrored,
        scratch=[
            pltpu.VMEM(stack_dims, BF16),
            pltpu.VMEM((tile_rows, channels, tile_cols), F32),
        ],
        flops=conv_flops,
        name="input_grad",
    )
    grad_weight, grad_bias = call(
        unpack_kernel,
        [shape((3, 3, channels, channels), F32), shape((1, channels), F32)],
        place[0],
        across,
        swapped(across),
        scratch=[packed],
        name="unpack",
    )
    mixed_keep, mixed_give = turn(held(mixed_arrived, across, *halo[:2]), place)
    symmetric = call(
        join_kernel,
        shape(pair_feature_map.shape, BF16),
        place[0],
        mixed_keep,
        swapped(mixed_give),
        *mixed,
        name="join",
    )
    return symmetric, grad_input, grad_weight, grad_bias.reshape(channels)


def solution(mesh):
    placed = (P(None, "row", "col"), P(), P(), P(None, "row", "col"))
    return jax.shard_map(
        shards,
        mesh=mesh,
        in_specs=placed,
        out_specs=(P(None, "row", "col"), P(None, "row", "col"), P(), P()),
        check_vma=False,
    )
```

```python
import functools

import jax
import jax.numpy as jnp
from jax import lax
from jax.experimental import pallas as pl
from jax.experimental.pallas import tpu as pltpu
from jax.sharding import PartitionSpec as P

DILATION_STEP = 8
STEP = DILATION_STEP
BF16, F32 = jnp.bfloat16, jnp.float32
VMEM_LIMIT = 24 * 1024 * 1024


def call(
    kernel, out_shape, *args, scratch=(), flops=0, in_hbm=(), out_hbm=0, aliases=None, name=None
):
    out_bytes = sum(o.size * o.dtype.itemsize for o in jax.tree.leaves(out_shape))
    in_bytes = sum(a.size * a.dtype.itemsize for a in args)
    in_specs = [
        pl.BlockSpec(memory_space=pltpu.SMEM if a.dtype == jnp.int32 else pltpu.VMEM) for a in args
    ]
    for k in in_hbm:
        in_specs[k] = pl.BlockSpec(memory_space=pl.ANY)
    out_specs = [pl.BlockSpec(memory_space=pltpu.VMEM)] * len(jax.tree.leaves(out_shape))
    if out_hbm:
        out_specs[-out_hbm:] = [pl.BlockSpec(memory_space=pl.ANY)] * out_hbm
    if not isinstance(out_shape, list):
        out_specs = out_specs[0]
    return pl.pallas_call(
        kernel,
        out_shape=out_shape,
        in_specs=in_specs,
        out_specs=out_specs,
        scratch_shapes=scratch,
        input_output_aliases=aliases or {},
        name=name,
        compiler_params=pltpu.CompilerParams(vmem_limit_bytes=VMEM_LIMIT),
        cost_estimate=pl.CostEstimate(
            flops=flops, bytes_accessed=in_bytes + out_bytes, transcendentals=0
        ),
    )(*args)


def shape(dims, dtype):
    return jax.ShapeDtypeStruct(tuple(dims), dtype)


def columns_of(rows, first):
    picked = [r[:, :STEP] if first else r[:, -STEP:] for r in rows]
    return jnp.concatenate(picked, axis=1)


def write_pair(parity, start, end, first, second):
    first[...] = jnp.where(parity == 0, end, start)
    second[...] = jnp.where(parity == 0, start, end)


def picked(parity, first, second):
    return jnp.where(parity == 0, second, first), jnp.where(parity == 0, first, second)


def write_edges(row_odd, col_odd, tile, top_ref, bottom_ref, first_ref, second_ref):
    tile_rows, _, tile_cols = tile.shape
    span = tile_cols // STEP
    for group in range(tile_rows // span):
        rows = [tile[group * span + k] for k in range(span)]
        write_pair(
            col_odd[0],
            columns_of(rows, True),
            columns_of(rows, False),
            first_ref.at[group],
            second_ref.at[group],
        )
    for k in range(STEP):
        top_ref[k] = tile[k]
        bottom_ref[k] = tile[tile_rows - STEP + k]


def edge_shapes(channels, tile_rows, tile_cols):
    rows = shape((STEP, channels, tile_cols), BF16)
    strips = shape((tile_rows * STEP // tile_cols, channels, tile_cols), BF16)
    return [rows, rows, strips, strips]


def exchanged(x, axis, turn):
    size = lax.axis_size(axis)
    pairs = [(i, i + 1) for i in range(turn, size - 1, 2)]
    return lax.ppermute(x, axis, pairs + [(j, i) for i, j in pairs])


def message_kernel(row_odd, col_odd, top, bottom, first, second, row_first, row_second):
    last = first.shape[0] - 1
    write_pair(row_odd[0], top[...], bottom[...], row_first.at[:STEP], row_second.at[:STEP])
    starts = picked(col_odd[0], first[0], second[0])
    ends = picked(col_odd[0], first[last], second[last])
    for k in range(2):
        write_pair(
            row_odd[0], starts[k], ends[k], row_first.at[STEP + k], row_second.at[STEP + k]
        )


def columns_of_halo(place, top, bottom, first, second):
    strips = exchanged(first, "col", 0), exchanged(second, "col", 1)
    message = shape((STEP + 2,) + top.shape[1:], BF16)
    rows = call(
        message_kernel, [message, message], *place, top, bottom, *strips, name="messages"
    )
    return rows, strips


def rows_of_halo(rows, *before_far):
    near = exchanged(rows[0], "row", 0)
    return near, exchanged(held(rows[1], near, *before_far), "row", 1)


def shifted(left, middle, right, lane, out):
    channels = middle.shape[0]
    left, right = left[:, lane : lane + STEP], right[:, lane : lane + STEP]
    out[:channels] = jnp.concatenate([left, middle[:, :-STEP]], axis=1)
    out[channels : 2 * channels] = middle
    out[2 * channels :] = jnp.concatenate([middle[:, STEP:], right], axis=1)


def write_own(col_odd, tile, col_first, col_second, stack):
    tile_rows, _, tile_cols = tile.shape
    span = tile_cols // STEP
    from_left, from_right = picked(col_odd[0], col_first[...], col_second[...])
    for row in range(tile_rows):
        group = row // span
        lane = STEP * (row % span)
        shifted(from_left[group], tile[row], from_right[group], lane, stack.at[STEP + row])


def write_ends(row_odd, row_first, row_second, before, after):
    span = row_first.shape[2] // STEP
    ends = picked(row_odd[0], row_first[...], row_second[...])
    for end, out, first in zip(ends, (before, after), (span - STEP, 0)):
        for k in range(STEP):
            shifted(end[STEP], end[k], end[STEP + 1], STEP * (first + k), out.at[k])


def write_shifted(row_odd, col_odd, tile, row_first, row_second, col_first, col_second, stack):
    write_own(col_odd, tile, col_first, col_second, stack)
    far = stack.shape[0] - STEP
    write_ends(row_odd, row_first, row_second, stack.at[:STEP], stack.at[far:])


def forward_taps(weight):
    lines = [jnp.concatenate([weight[p, q] for q in range(3)], axis=1) for p in range(3)]
    return jnp.concatenate(lines, axis=0)


def backward_taps(weight):
    lines = [
        jnp.concatenate([weight[2 - p, 2 - q].T for q in range(3)], axis=1) for p in range(3)
    ]
    return jnp.concatenate(lines, axis=0)


def convolve(stack, weights, tile_rows, emit):
    channels = weights.shape[0] // 3
    cols = stack.shape[2]
    for pair in range(STEP // 2):
        products = []
        for k in range(tile_rows // STEP + 2):
            row = STEP * k + 2 * pair
            both = jnp.concatenate([stack[row], stack[row + 1]], axis=1)
            products.append(jnp.dot(weights, both, preferred_element_type=F32))
            if k >= 2:
                total = (
                    products[k - 2][:channels]
                    + products[k - 1][channels : 2 * channels]
                    + products[k][2 * channels :]
                )
                out_row = STEP * (k - 2) + 2 * pair
                emit(out_row, total[:, :cols])
                emit(out_row + 1, total[:, cols:])


def open_kernel(row_odd, col_odd, cot, x, tile, top, bottom, first, second, *rest):
    pieces, done = rest[:-1], rest[-1]
    group = pieces[0].shape[0]
    copies = [
        pltpu.make_async_copy(cot.at[pl.ds(j * group, group)], piece, done.at[j])
        for j, piece in enumerate(pieces)
    ]
    for copy in copies:
        copy.start()
    rows = x.shape[1]
    for a in range(0, rows, 16):
        tile[a : a + 16] = jnp.swapaxes(x[:, a : a + 16], 0, 1)
    write_edges(row_odd, col_odd, tile, top, bottom, first, second)
    for copy in copies:
        copy.wait()


def forward_kernel(row_odd, col_odd, tile, *refs):
    halo, (weight, bias, token, stack, slope, *pieces, kept) = refs[:4], refs[4:]
    token[...] = jnp.zeros_like(token)
    group = pieces[0].shape[0]
    tile_rows = tile.shape[0]
    write_shifted(row_odd, col_odd, tile, *halo, stack)
    offset = bias[...]

    def emit(row, total):
        pre_act = total + offset
        rise = jnp.exp(jnp.minimum(pre_act, 0.0))
        slope[row] = rise
        elu = jnp.where(pre_act > 0, pre_act, rise - 1.0)
        kept[row] = (tile[row].astype(F32) + elu).astype(BF16)

    convolve(stack, forward_taps(weight), tile_rows, emit)
    for a in range(0, tile_rows, 16):
        mixed = jnp.swapaxes(kept[a : a + 16], 0, 1)
        for j, piece in enumerate(pieces):
            piece[:, a : a + 16] = mixed[j * group : (j + 1) * group]


def grad_pre_kernel(
    row_odd, col_odd, cot, keep, got, slope, token, tile, top, bottom, first, second, mirrored
):
    token[...] = jnp.zeros_like(token)
    rows = cot.shape[1]
    for a in range(0, rows, 16):
        turned = joined(row_odd[0], keep[:, a : a + 16], got[:, a : a + 16])
        mirrored[:, a : a + 16] = turned.astype(BF16)
        grad_mixed = cot[:, a : a + 16].astype(F32) + turned
        tile[a : a + 16] = (jnp.swapaxes(grad_mixed, 0, 1) * slope[a : a + 16]).astype(BF16)
    write_edges(row_odd, col_odd, tile, top, bottom, first, second)


def weight_kernel(side, row_odd, grad, stack, token, keep, give, packed):
    token[...] = jnp.zeros_like(token)
    tile_rows, channels, cols = grad.shape
    nothing = jnp.zeros((channels, cols), BF16)

    def taps(row):
        own = [row - STEP * p for p in range(3)]
        return jnp.concatenate([grad[a] if 0 <= a < tile_rows else nothing for a in own], axis=0)

    total = jnp.zeros((3 * channels, 3 * channels), F32)
    for row in range(0, tile_rows + 2 * STEP, 2):
        total = total + lax.dot_general(
            jnp.concatenate([taps(row), taps(row + 1)], axis=1),
            jnp.concatenate([stack[row], stack[row + 1]], axis=1),
            (((1,), (1,)), ((), ())),
            preferred_element_type=F32,
        )
    cells = jnp.zeros((channels, cols), F32)
    for row in range(tile_rows):
        cells = cells + grad[row].astype(F32)
    bias = jnp.broadcast_to(jnp.sum(cells, axis=1, keepdims=True), (channels, channels))
    blocks = [
        total[p * channels : (p + 1) * channels, q * channels : (q + 1) * channels]
        for p in range(3)
        for q in range(3)
    ] + [bias]
    for k in range(0, len(blocks), 2):
        at = k // 2 * channels
        packed[at : at + channels] = jnp.concatenate(blocks[k : k + 2], axis=1) * (1.0 / side)
    half = keep.shape[0]
    keep[...] = packed[pl.ds(row_odd[0] * half, half)]
    give[...] = packed[pl.ds((1 - row_odd[0]) * half, half)]


def unpack_kernel(row_odd, mine, other, weight, bias, packed):
    half, channels = mine.shape[0], weight.shape[2]
    packed[pl.ds(row_odd[0] * half, half)] = mine[...]
    packed[pl.ds((1 - row_odd[0]) * half, half)] = other[...]
    for k in range(9):
        row, col = k // 2 * channels, k % 2 * channels
        weight[k // 3, k % 3] = packed[row : row + channels, col : col + channels]
    last = packed[4 * channels :, channels:]
    line = lax.broadcasted_iota(jnp.int32, last.shape, 0)
    lane = lax.broadcasted_iota(jnp.int32, last.shape, 1)
    bias[...] = jnp.sum(jnp.where(line == lane, last, 0.0), axis=0, keepdims=True)


def input_grad_kernel(col_odd, tile, col_first, col_second, weight, cot, mirrored, *refs):
    token, out, ends, stack, kept = refs
    tile_rows = tile.shape[0]
    token[...] = jnp.zeros_like(token)
    for at in (0, tile_rows + STEP):
        stack[at : at + STEP] = jnp.zeros((STEP,) + stack.shape[1:], stack.dtype)
    write_own(col_odd, tile, col_first, col_second, stack)

    def emit(row, total):
        kept[row] = total

    convolve(stack, backward_taps(weight), tile_rows, emit)
    for a in range(0, tile_rows, 16):
        grad_mixed = cot[:, a : a + 16].astype(F32) + mirrored[:, a : a + 16].astype(F32)
        total = grad_mixed + jnp.swapaxes(kept[a : a + 16], 0, 1)
        if a == 0:
            ends[0] = total
        elif a == tile_rows - 16:
            ends[1] = total
        else:
            out[:, a : a + 16] = total.astype(BF16)


def input_grad_ends_kernel(row_odd, row_first, row_second, weight, ends, whole, out, *scratch):
    before, after, added, rounded, done = scratch
    channels, tile_rows = out.shape[:2]
    taps = backward_taps(weight)
    write_ends(row_odd, row_first, row_second, before, after)
    added[...] = jnp.zeros_like(added)
    for side, rows, tap, at in ((0, before, 0, 0), (1, after, 2, STEP)):
        own = taps[tap * channels : (tap + 1) * channels]
        for k in range(0, STEP, 2):
            both = jnp.concatenate([rows[k], rows[k + 1]], axis=1)
            total = jnp.dot(own, both, preferred_element_type=F32)
            cols = total.shape[1] // 2
            added[side, at + k] = total[:, :cols]
            added[side, at + k + 1] = total[:, cols:]
    copies = []
    for side, a in ((0, 0), (1, tile_rows - 16)):
        total = ends[side] + jnp.swapaxes(added[side], 0, 1)
        rounded[side] = total.astype(BF16)
        copy = pltpu.make_async_copy(
            rounded.at[side], out.at[:, pl.ds(a, 16)], done.at[side]
        )
        copy.start()
        copies.append(copy)
    for copy in copies:
        copy.wait()


def turn_kernel(unread, row_odd, *refs):
    pieces, (keep, give) = refs[unread:-2], refs[-2:]
    tile_rows = pieces[0].shape[1]
    core = row_odd[0]
    group, near = pieces[0].shape[0], len(pieces) // 2
    for j in range(near):
        for c in range(group):
            low, high = pieces[j][c].T, pieces[j + near][c].T
            first = jnp.concatenate([low[:tile_rows], high[:tile_rows]], axis=1)
            second = jnp.concatenate([low[tile_rows:], high[tile_rows:]], axis=1)
            keep[j * group + c] = jnp.where(core == 0, first, second)
            give[j * group + c] = jnp.where(core == 0, second, first)


def joined(core, keep, got):
    lower = lax.broadcasted_iota(jnp.int32, (1, 1, keep.shape[2]), 2) < keep.shape[2] // 2
    keep, got = keep.astype(F32), got.astype(F32)
    first, second = jnp.where(core == 0, keep, got), jnp.where(core == 0, got, keep)
    low = jnp.where(lower, first, pltpu.roll(second, keep.shape[2] // 2, 2))
    high = jnp.where(lower, pltpu.roll(first, keep.shape[2] // 2, 2), second)
    return jnp.concatenate([low, high], axis=0)


def detour(piece, far):
    if far == 0:
        return piece
    return lax.ppermute(piece, "row", [(r, r ^ (2 * far)) for r in range(lax.axis_size("row"))])


def cross(piece, far):
    size, blocks = lax.axis_size("row"), lax.axis_size("col")
    owners = [
        (r * blocks + z, (z * 2 + r % 2) * blocks + ((r // 2) ^ far))
        for r in range(size)
        for z in range(blocks)
    ]
    return lax.ppermute(piece, ("row", "col"), owners)


def turn(pieces, place, *after):
    group, tile_rows, tile_cols = pieces[0].shape
    half = shape((group * len(pieces) // 2, tile_rows, tile_cols), BF16)
    kernel = functools.partial(turn_kernel, len(after))
    return call(kernel, [half, half], place[0], *after, *pieces, name="turn")


def swapped(give):
    return lax.ppermute(give, "row", [(r, r ^ 1) for r in range(lax.axis_size("row"))])


def held(pieces, *until):
    return lax.optimization_barrier((pieces, until))[0]


def join_kernel(row_odd, keep, got, *refs):
    pieces, out = refs[:-1], refs[-1]
    for a in range(0, out.shape[1], 16):
        rows = slice(a, a + 16)
        turned = joined(row_odd[0], keep[:, rows], got[:, rows])
        own = jnp.concatenate([piece[:, rows] for piece in pieces], axis=0)
        out[:, rows] = (own.astype(F32) + turned).astype(BF16)


def summed(part, axis, reach):
    size = lax.axis_size(axis)
    while reach < size:
        part = part + lax.ppermute(part, axis, [(i, i ^ reach) for i in range(size)])
        reach *= 2
    return part


def shards(pair_feature_map, conv_weight, conv_bias, cotangent):
    channels, tile_rows, tile_cols = pair_feature_map.shape
    side = tile_rows * lax.axis_size("row")
    tile_shape = shape((tile_rows, channels, tile_cols), BF16)
    edges = edge_shapes(channels, tile_rows, tile_cols)
    stack_dims = (tile_rows + 2 * STEP, 3 * channels, tile_cols)
    conv_flops = 2 * 9 * channels * channels * tile_rows * tile_cols
    rounds = lax.axis_size("col")
    place = [jnp.full((1,), lax.axis_index(axis) % 2, jnp.int32) for axis in ("row", "col")]
    piece = shape((channels // rounds, tile_rows, tile_cols), BF16)

    tile, *opened = call(
        open_kernel,
        [tile_shape] + edges + [piece] * rounds,
        *place,
        cotangent,
        pair_feature_map,
        scratch=[pltpu.SemaphoreType.DMA((rounds,))],
        in_hbm=[2],
        out_hbm=rounds,
        name="open",
    )
    token = shape((8, 128), F32)
    dealt = [detour(p, j) for j, p in enumerate(opened[4:])]
    rows, strips = columns_of_halo(place, *opened[:4])
    halo = *rows_of_halo(rows), *strips
    forwarded, stack, slope, *mixed = call(
        forward_kernel,
        [token, shape(stack_dims, BF16), shape((tile_rows, channels, tile_cols), F32)]
        + [piece] * rounds,
        *place,
        tile,
        *halo,
        conv_weight,
        conv_bias[:, None],
        scratch=[pltpu.VMEM((tile_rows, channels, tile_cols), BF16)],
        flops=conv_flops,
        name="forward",
    )
    arrived = [cross(held(p, *halo[2:]), j) for j, p in enumerate(dealt)]
    mixed_dealt = [detour(p, j) for j, p in enumerate(mixed)]
    keep, give = turn(held(arrived, slope), place)
    ready, grad, *edge, mirrored = call(
        grad_pre_kernel,
        [token, tile_shape] + edges + [shape(cotangent.shape, BF16)],
        *place,
        cotangent,
        keep,
        swapped(give),
        slope,
        name="grad_pre",
    )
    packed = pltpu.VMEM((5 * channels, 2 * channels), F32)
    half = shape((5 * channels // 2, 2 * channels), F32)
    weighed, *terms = call(
        functools.partial(weight_kernel, side),
        [token, half, half],
        place[0],
        grad,
        stack,
        scratch=[packed],
        flops=conv_flops,
        name="weight_terms",
    )
    part = held(terms[0] + swapped(terms[1]), mixed_dealt[1])
    size = lax.axis_size("col")
    part = part + lax.ppermute(part, "col", [(i, i ^ 1) for i in range(size)])
    part = summed(held(part, mixed_dealt[2]), "col", 2)
    across = summed(part, "row", 2)
    rows, strips = columns_of_halo(place, *edge)
    mixed_arrived = [cross(held(p, part), j) for j, p in enumerate(mixed_dealt)]
    ended, grad_input, ends = call(
        input_grad_kernel,
        [token, shape(cotangent.shape, BF16), shape((2, channels, 16, tile_cols), F32)],
        place[1],
        grad,
        *strips,
        conv_weight,
        cotangent,
        mirrored,
        scratch=[
            pltpu.VMEM(stack_dims, BF16),
            pltpu.VMEM((tile_rows, channels, tile_cols), F32),
        ],
        flops=conv_flops,
        name="input_grad",
    )
    halo = rows_of_halo(rows, ended)
    strip = pltpu.VMEM((STEP, 3 * channels, tile_cols), BF16)
    grad_input = call(
        input_grad_ends_kernel,
        shape(cotangent.shape, BF16),
        place[0],
        *halo,
        conv_weight,
        ends,
        grad_input,
        scratch=[
            strip,
            strip,
            pltpu.VMEM((2, 16, channels, tile_cols), F32),
            pltpu.VMEM((2, channels, 16, tile_cols), BF16),
            pltpu.SemaphoreType.DMA((2,)),
        ],
        in_hbm=[5],
        out_hbm=1,
        aliases={5: 0},
        name="input_grad_ends",
    )
    grad_weight, grad_bias = call(
        unpack_kernel,
        [shape((3, 3, channels, channels), F32), shape((1, channels), F32)],
        place[0],
        across,
        swapped(across),
        scratch=[packed],
        name="unpack",
    )
    mixed_keep, mixed_give = turn(held(mixed_arrived, across, *halo), place, ended)
    symmetric = call(
        join_kernel,
        shape(pair_feature_map.shape, BF16),
        place[0],
        mixed_keep,
        swapped(mixed_give),
        *mixed,
        name="join",
    )
    return symmetric, grad_input, grad_weight, grad_bias.reshape(channels)


def solution(mesh):
    placed = (P(None, "row", "col"), P(), P(), P(None, "row", "col"))
    return jax.shard_map(
        shards,
        mesh=mesh,
        in_specs=placed,
        out_specs=(P(None, "row", "col"), P(None, "row", "col"), P(), P()),
        check_vma=False,
    )
```

```python
import functools

import jax
import jax.numpy as jnp
from jax import lax
from jax.experimental import pallas as pl
from jax.experimental.pallas import tpu as pltpu
from jax.sharding import PartitionSpec as P

DILATION_STEP = 8
STEP = DILATION_STEP
BF16, F32 = jnp.bfloat16, jnp.float32
VMEM_LIMIT = 24 * 1024 * 1024


def call(
    kernel, out_shape, *args, scratch=(), flops=0, in_hbm=(), out_hbm=0, aliases=None, name=None
):
    out_bytes = sum(o.size * o.dtype.itemsize for o in jax.tree.leaves(out_shape))
    in_bytes = sum(a.size * a.dtype.itemsize for a in args)
    in_specs = [
        pl.BlockSpec(memory_space=pltpu.SMEM if a.dtype == jnp.int32 else pltpu.VMEM) for a in args
    ]
    for k in in_hbm:
        in_specs[k] = pl.BlockSpec(memory_space=pl.ANY)
    out_specs = [pl.BlockSpec(memory_space=pltpu.VMEM)] * len(jax.tree.leaves(out_shape))
    if out_hbm:
        out_specs[-out_hbm:] = [pl.BlockSpec(memory_space=pl.ANY)] * out_hbm
    if not isinstance(out_shape, list):
        out_specs = out_specs[0]
    return pl.pallas_call(
        kernel,
        out_shape=out_shape,
        in_specs=in_specs,
        out_specs=out_specs,
        scratch_shapes=scratch,
        input_output_aliases=aliases or {},
        name=name,
        compiler_params=pltpu.CompilerParams(vmem_limit_bytes=VMEM_LIMIT),
        cost_estimate=pl.CostEstimate(
            flops=flops, bytes_accessed=in_bytes + out_bytes, transcendentals=0
        ),
    )(*args)


def shape(dims, dtype):
    return jax.ShapeDtypeStruct(tuple(dims), dtype)


def columns_of(rows, first):
    picked = [r[:, :STEP] if first else r[:, -STEP:] for r in rows]
    return jnp.concatenate(picked, axis=1)


def write_pair(parity, start, end, first, second):
    first[...] = jnp.where(parity == 0, end, start)
    second[...] = jnp.where(parity == 0, start, end)


def picked(parity, first, second):
    return jnp.where(parity == 0, second, first), jnp.where(parity == 0, first, second)


def write_edges(row_odd, col_odd, tile, top_ref, bottom_ref, first_ref, second_ref):
    tile_rows, _, tile_cols = tile.shape
    span = tile_cols // STEP
    for group in range(tile_rows // span):
        rows = [tile[group * span + k] for k in range(span)]
        write_pair(
            col_odd[0],
            columns_of(rows, True),
            columns_of(rows, False),
            first_ref.at[group],
            second_ref.at[group],
        )
    for k in range(STEP):
        top_ref[k] = tile[k]
        bottom_ref[k] = tile[tile_rows - STEP + k]


def edge_shapes(channels, tile_rows, tile_cols):
    rows = shape((STEP, channels, tile_cols), BF16)
    strips = shape((tile_rows * STEP // tile_cols, channels, tile_cols), BF16)
    return [rows, rows, strips, strips]


def exchanged(x, axis, turn):
    size = lax.axis_size(axis)
    pairs = [(i, i + 1) for i in range(turn, size - 1, 2)]
    return lax.ppermute(x, axis, pairs + [(j, i) for i, j in pairs])


def message_kernel(row_odd, col_odd, top, bottom, first, second, row_first, row_second):
    last = first.shape[0] - 1
    write_pair(row_odd[0], top[...], bottom[...], row_first.at[:STEP], row_second.at[:STEP])
    starts = picked(col_odd[0], first[0], second[0])
    ends = picked(col_odd[0], first[last], second[last])
    for k in range(2):
        write_pair(
            row_odd[0], starts[k], ends[k], row_first.at[STEP + k], row_second.at[STEP + k]
        )


def columns_of_halo(place, top, bottom, first, second):
    strips = exchanged(first, "col", 0), exchanged(second, "col", 1)
    message = shape((STEP + 2,) + top.shape[1:], BF16)
    rows = call(
        message_kernel, [message, message], *place, top, bottom, *strips, name="messages"
    )
    return rows, strips


def rows_of_halo(rows):
    near = exchanged(rows[0], "row", 0)
    return near, exchanged(held(rows[1], near), "row", 1)


def shifted(left, middle, right, lane, out):
    channels = middle.shape[0]
    left, right = left[:, lane : lane + STEP], right[:, lane : lane + STEP]
    out[:channels] = jnp.concatenate([left, middle[:, :-STEP]], axis=1)
    out[channels : 2 * channels] = middle
    out[2 * channels :] = jnp.concatenate([middle[:, STEP:], right], axis=1)


def write_own(col_odd, tile, col_first, col_second, stack):
    tile_rows, _, tile_cols = tile.shape
    span = tile_cols // STEP
    from_left, from_right = picked(col_odd[0], col_first[...], col_second[...])
    for row in range(tile_rows):
        group = row // span
        lane = STEP * (row % span)
        shifted(from_left[group], tile[row], from_right[group], lane, stack.at[STEP + row])


def write_ends(row_odd, row_first, row_second, before, after):
    span = row_first.shape[2] // STEP
    ends = picked(row_odd[0], row_first[...], row_second[...])
    for end, out, first in zip(ends, (before, after), (span - STEP, 0)):
        for k in range(STEP):
            shifted(end[STEP], end[k], end[STEP + 1], STEP * (first + k), out.at[k])


def write_shifted(row_odd, col_odd, tile, row_first, row_second, col_first, col_second, stack):
    write_own(col_odd, tile, col_first, col_second, stack)
    far = stack.shape[0] - STEP
    write_ends(row_odd, row_first, row_second, stack.at[:STEP], stack.at[far:])


def forward_taps(weight):
    lines = [jnp.concatenate([weight[p, q] for q in range(3)], axis=1) for p in range(3)]
    return jnp.concatenate(lines, axis=0)


def backward_taps(weight):
    lines = [
        jnp.concatenate([weight[2 - p, 2 - q].T for q in range(3)], axis=1) for p in range(3)
    ]
    return jnp.concatenate(lines, axis=0)


def convolve(stack, weights, tile_rows, emit):
    channels = weights.shape[0] // 3
    cols = stack.shape[2]
    for pair in range(STEP // 2):
        products = []
        for k in range(tile_rows // STEP + 2):
            row = STEP * k + 2 * pair
            both = jnp.concatenate([stack[row], stack[row + 1]], axis=1)
            products.append(jnp.dot(weights, both, preferred_element_type=F32))
            if k >= 2:
                total = (
                    products[k - 2][:channels]
                    + products[k - 1][channels : 2 * channels]
                    + products[k][2 * channels :]
                )
                out_row = STEP * (k - 2) + 2 * pair
                emit(out_row, total[:, :cols])
                emit(out_row + 1, total[:, cols:])


def open_kernel(row_odd, col_odd, cot, x, tile, top, bottom, first, second, *rest):
    pieces, done = rest[:-1], rest[-1]
    group = pieces[0].shape[0]
    copies = [
        pltpu.make_async_copy(cot.at[pl.ds(j * group, group)], piece, done.at[j])
        for j, piece in enumerate(pieces)
    ]
    for copy in copies:
        copy.start()
    rows = x.shape[1]
    for a in range(0, rows, 16):
        tile[a : a + 16] = jnp.swapaxes(x[:, a : a + 16], 0, 1)
    write_edges(row_odd, col_odd, tile, top, bottom, first, second)
    for copy in copies:
        copy.wait()


def forward_kernel(row_odd, col_odd, tile, *refs):
    halo, (weight, bias, token, stack, slope, *pieces, kept) = refs[:4], refs[4:]
    token[...] = jnp.zeros_like(token)
    group = pieces[0].shape[0]
    tile_rows = tile.shape[0]
    write_shifted(row_odd, col_odd, tile, *halo, stack)
    offset = bias[...]

    def emit(row, total):
        pre_act = total + offset
        rise = jnp.exp(jnp.minimum(pre_act, 0.0))
        slope[row] = rise
        elu = jnp.where(pre_act > 0, pre_act, rise - 1.0)
        kept[row] = (tile[row].astype(F32) + elu).astype(BF16)

    convolve(stack, forward_taps(weight), tile_rows, emit)
    for a in range(0, tile_rows, 16):
        mixed = jnp.swapaxes(kept[a : a + 16], 0, 1)
        for j, piece in enumerate(pieces):
            piece[:, a : a + 16] = mixed[j * group : (j + 1) * group]


def grad_pre_kernel(
    row_odd, col_odd, cot, keep, got, slope, token, tile, top, bottom, first, second, mirrored
):
    token[...] = jnp.zeros_like(token)
    rows = cot.shape[1]
    for a in range(0, rows, 16):
        turned = joined(row_odd[0], keep[:, a : a + 16], got[:, a : a + 16])
        mirrored[:, a : a + 16] = turned.astype(BF16)
        grad_mixed = cot[:, a : a + 16].astype(F32) + turned
        tile[a : a + 16] = (jnp.swapaxes(grad_mixed, 0, 1) * slope[a : a + 16]).astype(BF16)
    write_edges(row_odd, col_odd, tile, top, bottom, first, second)


def weight_kernel(side, row_odd, grad, stack, token, keep, give, packed):
    token[...] = jnp.zeros_like(token)
    tile_rows, channels, cols = grad.shape
    nothing = jnp.zeros((channels, cols), BF16)

    def taps(row):
        own = [row - STEP * p for p in range(3)]
        return jnp.concatenate([grad[a] if 0 <= a < tile_rows else nothing for a in own], axis=0)

    total = jnp.zeros((3 * channels, 3 * channels), F32)
    for row in range(0, tile_rows + 2 * STEP, 2):
        total = total + lax.dot_general(
            jnp.concatenate([taps(row), taps(row + 1)], axis=1),
            jnp.concatenate([stack[row], stack[row + 1]], axis=1),
            (((1,), (1,)), ((), ())),
            preferred_element_type=F32,
        )
    cells = jnp.zeros((channels, cols), F32)
    for row in range(tile_rows):
        cells = cells + grad[row].astype(F32)
    bias = jnp.broadcast_to(jnp.sum(cells, axis=1, keepdims=True), (channels, channels))
    blocks = [
        total[p * channels : (p + 1) * channels, q * channels : (q + 1) * channels]
        for p in range(3)
        for q in range(3)
    ] + [bias]
    for k in range(0, len(blocks), 2):
        at = k // 2 * channels
        packed[at : at + channels] = jnp.concatenate(blocks[k : k + 2], axis=1) * (1.0 / side)
    half = keep.shape[0]
    keep[...] = packed[pl.ds(row_odd[0] * half, half)]
    give[...] = packed[pl.ds((1 - row_odd[0]) * half, half)]


def unpack_kernel(row_odd, mine, other, weight, bias, packed):
    half, channels = mine.shape[0], weight.shape[2]
    packed[pl.ds(row_odd[0] * half, half)] = mine[...]
    packed[pl.ds((1 - row_odd[0]) * half, half)] = other[...]
    for k in range(9):
        row, col = k // 2 * channels, k % 2 * channels
        weight[k // 3, k % 3] = packed[row : row + channels, col : col + channels]
    last = packed[4 * channels :, channels:]
    line = lax.broadcasted_iota(jnp.int32, last.shape, 0)
    lane = lax.broadcasted_iota(jnp.int32, last.shape, 1)
    bias[...] = jnp.sum(jnp.where(line == lane, last, 0.0), axis=0, keepdims=True)


def input_grad_kernel(col_odd, tile, col_first, col_second, weight, cot, mirrored, *refs):
    token, out, ends, stack, kept = refs
    tile_rows = tile.shape[0]
    token[...] = jnp.zeros_like(token)
    for at in (0, tile_rows + STEP):
        stack[at : at + STEP] = jnp.zeros((STEP,) + stack.shape[1:], stack.dtype)
    write_own(col_odd, tile, col_first, col_second, stack)

    def emit(row, total):
        kept[row] = total

    convolve(stack, backward_taps(weight), tile_rows, emit)
    for a in range(0, tile_rows, 16):
        grad_mixed = cot[:, a : a + 16].astype(F32) + mirrored[:, a : a + 16].astype(F32)
        total = grad_mixed + jnp.swapaxes(kept[a : a + 16], 0, 1)
        if a == 0:
            ends[0] = total
        elif a == tile_rows - 16:
            ends[1] = total
        else:
            out[:, a : a + 16] = total.astype(BF16)


def input_grad_ends_kernel(row_odd, row_first, row_second, weight, ends, whole, out, *scratch):
    before, after, added, rounded, done = scratch
    channels, tile_rows = out.shape[:2]
    taps = backward_taps(weight)
    write_ends(row_odd, row_first, row_second, before, after)
    added[...] = jnp.zeros_like(added)
    for side, rows, tap, at in ((0, before, 0, 0), (1, after, 2, STEP)):
        own = taps[tap * channels : (tap + 1) * channels]
        for k in range(0, STEP, 2):
            both = jnp.concatenate([rows[k], rows[k + 1]], axis=1)
            total = jnp.dot(own, both, preferred_element_type=F32)
            cols = total.shape[1] // 2
            added[side, at + k] = total[:, :cols]
            added[side, at + k + 1] = total[:, cols:]
    copies = []
    for side, a in ((0, 0), (1, tile_rows - 16)):
        total = ends[side] + jnp.swapaxes(added[side], 0, 1)
        rounded[side] = total.astype(BF16)
        copy = pltpu.make_async_copy(
            rounded.at[side], out.at[:, pl.ds(a, 16)], done.at[side]
        )
        copy.start()
        copies.append(copy)
    for copy in copies:
        copy.wait()


def turn_kernel(unread, row_odd, *refs):
    pieces, (keep, give) = refs[unread:-2], refs[-2:]
    tile_rows = pieces[0].shape[1]
    core = row_odd[0]
    group, near = pieces[0].shape[0], len(pieces) // 2
    for j in range(near):
        for c in range(group):
            low, high = pieces[j][c].T, pieces[j + near][c].T
            first = jnp.concatenate([low[:tile_rows], high[:tile_rows]], axis=1)
            second = jnp.concatenate([low[tile_rows:], high[tile_rows:]], axis=1)
            keep[j * group + c] = jnp.where(core == 0, first, second)
            give[j * group + c] = jnp.where(core == 0, second, first)


def joined(core, keep, got):
    lower = lax.broadcasted_iota(jnp.int32, (1, 1, keep.shape[2]), 2) < keep.shape[2] // 2
    keep, got = keep.astype(F32), got.astype(F32)
    first, second = jnp.where(core == 0, keep, got), jnp.where(core == 0, got, keep)
    low = jnp.where(lower, first, pltpu.roll(second, keep.shape[2] // 2, 2))
    high = jnp.where(lower, pltpu.roll(first, keep.shape[2] // 2, 2), second)
    return jnp.concatenate([low, high], axis=0)


def detour(piece, far):
    if far == 0:
        return piece
    return lax.ppermute(piece, "row", [(r, r ^ (2 * far)) for r in range(lax.axis_size("row"))])


def cross(piece, far):
    size, blocks = lax.axis_size("row"), lax.axis_size("col")
    owners = [
        (r * blocks + z, (z * 2 + r % 2) * blocks + ((r // 2) ^ far))
        for r in range(size)
        for z in range(blocks)
    ]
    return lax.ppermute(piece, ("row", "col"), owners)


def turn(pieces, place, *after):
    group, tile_rows, tile_cols = pieces[0].shape
    half = shape((group * len(pieces) // 2, tile_rows, tile_cols), BF16)
    kernel = functools.partial(turn_kernel, len(after))
    return call(kernel, [half, half], place[0], *after, *pieces, name="turn")


def swapped(give):
    return lax.ppermute(give, "row", [(r, r ^ 1) for r in range(lax.axis_size("row"))])


def held(pieces, *until):
    return lax.optimization_barrier((pieces, until))[0]


def join_kernel(row_odd, keep, got, *refs):
    pieces, out = refs[:-1], refs[-1]
    for a in range(0, out.shape[1], 16):
        rows = slice(a, a + 16)
        turned = joined(row_odd[0], keep[:, rows], got[:, rows])
        own = jnp.concatenate([piece[:, rows] for piece in pieces], axis=0)
        out[:, rows] = (own.astype(F32) + turned).astype(BF16)


def summed(part, axis, reach):
    size = lax.axis_size(axis)
    while reach < size:
        part = part + lax.ppermute(part, axis, [(i, i ^ reach) for i in range(size)])
        reach *= 2
    return part


def shards(pair_feature_map, conv_weight, conv_bias, cotangent):
    channels, tile_rows, tile_cols = pair_feature_map.shape
    side = tile_rows * lax.axis_size("row")
    tile_shape = shape((tile_rows, channels, tile_cols), BF16)
    edges = edge_shapes(channels, tile_rows, tile_cols)
    stack_dims = (tile_rows + 2 * STEP, 3 * channels, tile_cols)
    conv_flops = 2 * 9 * channels * channels * tile_rows * tile_cols
    rounds = lax.axis_size("col")
    place = [jnp.full((1,), lax.axis_index(axis) % 2, jnp.int32) for axis in ("row", "col")]
    piece = shape((channels // rounds, tile_rows, tile_cols), BF16)

    tile, *opened = call(
        open_kernel,
        [tile_shape] + edges + [piece] * rounds,
        *place,
        cotangent,
        pair_feature_map,
        scratch=[pltpu.SemaphoreType.DMA((rounds,))],
        in_hbm=[2],
        out_hbm=rounds,
        name="open",
    )
    token = shape((8, 128), F32)
    dealt = [detour(p, j) for j, p in enumerate(opened[4:])]
    rows, strips = columns_of_halo(place, *opened[:4])
    halo = *rows_of_halo(rows), *strips
    forwarded, stack, slope, *mixed = call(
        forward_kernel,
        [token, shape(stack_dims, BF16), shape((tile_rows, channels, tile_cols), F32)]
        + [piece] * rounds,
        *place,
        tile,
        *halo,
        conv_weight,
        conv_bias[:, None],
        scratch=[pltpu.VMEM((tile_rows, channels, tile_cols), BF16)],
        flops=conv_flops,
        name="forward",
    )
    arrived = [cross(held(p, halo[2]), j) for j, p in enumerate(dealt)]
    mixed_dealt = [detour(p, j) for j, p in enumerate(mixed)]
    keep, give = turn(held(arrived, slope), place)
    ready, grad, *edge, mirrored = call(
        grad_pre_kernel,
        [token, tile_shape] + edges + [shape(cotangent.shape, BF16)],
        *place,
        cotangent,
        keep,
        swapped(give),
        slope,
        name="grad_pre",
    )
    packed = pltpu.VMEM((5 * channels, 2 * channels), F32)
    half = shape((5 * channels // 2, 2 * channels), F32)
    weighed, *terms = call(
        functools.partial(weight_kernel, side),
        [token, half, half],
        place[0],
        grad,
        stack,
        scratch=[packed],
        flops=conv_flops,
        name="weight_terms",
    )
    part = held(terms[0] + swapped(terms[1]), mixed_dealt[1])
    size = lax.axis_size("col")
    part = part + lax.ppermute(part, "col", [(i, i ^ 1) for i in range(size)])
    part = summed(held(part, mixed_dealt[2]), "col", 2)
    across = summed(part, "row", 2)
    rows, strips = columns_of_halo(place, *edge)
    mixed_arrived = [cross(held(p, part, *strips), j) for j, p in enumerate(mixed_dealt)]
    ended, grad_input, ends = call(
        input_grad_kernel,
        [token, shape(cotangent.shape, BF16), shape((2, channels, 16, tile_cols), F32)],
        place[1],
        grad,
        *strips,
        conv_weight,
        cotangent,
        mirrored,
        scratch=[
            pltpu.VMEM(stack_dims, BF16),
            pltpu.VMEM((tile_rows, channels, tile_cols), F32),
        ],
        flops=conv_flops,
        name="input_grad",
    )
    halo = rows_of_halo(rows)
    strip = pltpu.VMEM((STEP, 3 * channels, tile_cols), BF16)
    grad_input = call(
        input_grad_ends_kernel,
        shape(cotangent.shape, BF16),
        place[0],
        *halo,
        conv_weight,
        ends,
        grad_input,
        scratch=[
            strip,
            strip,
            pltpu.VMEM((2, 16, channels, tile_cols), F32),
            pltpu.VMEM((2, channels, 16, tile_cols), BF16),
            pltpu.SemaphoreType.DMA((2,)),
        ],
        in_hbm=[5],
        out_hbm=1,
        aliases={5: 0},
        name="input_grad_ends",
    )
    grad_weight, grad_bias = call(
        unpack_kernel,
        [shape((3, 3, channels, channels), F32), shape((1, channels), F32)],
        place[0],
        across,
        swapped(across),
        scratch=[packed],
        name="unpack",
    )
    mixed_keep, mixed_give = turn(held(mixed_arrived, across, *halo), place, ended)
    symmetric = call(
        join_kernel,
        shape(pair_feature_map.shape, BF16),
        place[0],
        mixed_keep,
        swapped(mixed_give),
        *mixed,
        name="join",
    )
    return symmetric, grad_input, grad_weight, grad_bias.reshape(channels)


def solution(mesh):
    placed = (P(None, "row", "col"), P(), P(), P(None, "row", "col"))
    return jax.shard_map(
        shards,
        mesh=mesh,
        in_specs=placed,
        out_specs=(P(None, "row", "col"), P(None, "row", "col"), P(), P()),
        check_vma=False,
    )
```

```python
import functools

import jax
import jax.numpy as jnp
from jax import lax
from jax.experimental import pallas as pl
from jax.experimental.pallas import tpu as pltpu
from jax.sharding import PartitionSpec as P

DILATION_STEP = 8
STEP = DILATION_STEP
BF16, F32 = jnp.bfloat16, jnp.float32
VMEM_LIMIT = 24 * 1024 * 1024


def call(
    kernel, out_shape, *args, scratch=(), flops=0, in_hbm=(), out_hbm=0, aliases=None, name=None
):
    out_bytes = sum(o.size * o.dtype.itemsize for o in jax.tree.leaves(out_shape))
    in_bytes = sum(a.size * a.dtype.itemsize for a in args)
    in_specs = [
        pl.BlockSpec(memory_space=pltpu.SMEM if a.dtype == jnp.int32 else pltpu.VMEM) for a in args
    ]
    for k in in_hbm:
        in_specs[k] = pl.BlockSpec(memory_space=pl.ANY)
    out_specs = [pl.BlockSpec(memory_space=pltpu.VMEM)] * len(jax.tree.leaves(out_shape))
    if out_hbm:
        out_specs[-out_hbm:] = [pl.BlockSpec(memory_space=pl.ANY)] * out_hbm
    if not isinstance(out_shape, list):
        out_specs = out_specs[0]
    return pl.pallas_call(
        kernel,
        out_shape=out_shape,
        in_specs=in_specs,
        out_specs=out_specs,
        scratch_shapes=scratch,
        input_output_aliases=aliases or {},
        name=name,
        compiler_params=pltpu.CompilerParams(vmem_limit_bytes=VMEM_LIMIT),
        cost_estimate=pl.CostEstimate(
            flops=flops, bytes_accessed=in_bytes + out_bytes, transcendentals=0
        ),
    )(*args)


def shape(dims, dtype):
    return jax.ShapeDtypeStruct(tuple(dims), dtype)


def columns_of(rows, first):
    picked = [r[:, :STEP] if first else r[:, -STEP:] for r in rows]
    return jnp.concatenate(picked, axis=1)


def write_pair(parity, start, end, first, second):
    first[...] = jnp.where(parity == 0, end, start)
    second[...] = jnp.where(parity == 0, start, end)


def picked(parity, first, second):
    return jnp.where(parity == 0, second, first), jnp.where(parity == 0, first, second)


def write_edges(row_odd, col_odd, tile, top_ref, bottom_ref, first_ref, second_ref):
    tile_rows, _, tile_cols = tile.shape
    span = tile_cols // STEP
    for group in range(tile_rows // span):
        rows = [tile[group * span + k] for k in range(span)]
        write_pair(
            col_odd[0],
            columns_of(rows, True),
            columns_of(rows, False),
            first_ref.at[group],
            second_ref.at[group],
        )
    for k in range(STEP):
        top_ref[k] = tile[k]
        bottom_ref[k] = tile[tile_rows - STEP + k]


def edge_shapes(channels, tile_rows, tile_cols):
    rows = shape((STEP, channels, tile_cols), BF16)
    strips = shape((tile_rows * STEP // tile_cols, channels, tile_cols), BF16)
    return [rows, rows, strips, strips]


def exchanged(x, axis, turn):
    size = lax.axis_size(axis)
    pairs = [(i, i + 1) for i in range(turn, size - 1, 2)]
    return lax.ppermute(x, axis, pairs + [(j, i) for i, j in pairs])


def message_kernel(row_odd, col_odd, top, bottom, first, second, row_first, row_second):
    last = first.shape[0] - 1
    write_pair(row_odd[0], top[...], bottom[...], row_first.at[:STEP], row_second.at[:STEP])
    starts = picked(col_odd[0], first[0], second[0])
    ends = picked(col_odd[0], first[last], second[last])
    for k in range(2):
        write_pair(
            row_odd[0], starts[k], ends[k], row_first.at[STEP + k], row_second.at[STEP + k]
        )


def columns_of_halo(place, top, bottom, first, second):
    strips = exchanged(first, "col", 0), exchanged(second, "col", 1)
    message = shape((STEP + 2,) + top.shape[1:], BF16)
    rows = call(
        message_kernel, [message, message], *place, top, bottom, *strips, name="messages"
    )
    return rows, strips


def rows_of_halo(rows):
    near = exchanged(rows[0], "row", 0)
    return near, exchanged(held(rows[1], near), "row", 1)


def shifted(left, middle, right, lane, out):
    channels = middle.shape[0]
    left, right = left[:, lane : lane + STEP], right[:, lane : lane + STEP]
    out[:channels] = jnp.concatenate([left, middle[:, :-STEP]], axis=1)
    out[channels : 2 * channels] = middle
    out[2 * channels :] = jnp.concatenate([middle[:, STEP:], right], axis=1)


def write_own(col_odd, tile, col_first, col_second, stack):
    tile_rows, _, tile_cols = tile.shape
    span = tile_cols // STEP
    from_left, from_right = picked(col_odd[0], col_first[...], col_second[...])
    for row in range(tile_rows):
        group = row // span
        lane = STEP * (row % span)
        shifted(from_left[group], tile[row], from_right[group], lane, stack.at[STEP + row])


def write_ends(row_odd, row_first, row_second, before, after):
    span = row_first.shape[2] // STEP
    ends = picked(row_odd[0], row_first[...], row_second[...])
    for end, out, first in zip(ends, (before, after), (span - STEP, 0)):
        for k in range(STEP):
            shifted(end[STEP], end[k], end[STEP + 1], STEP * (first + k), out.at[k])


def write_shifted(row_odd, col_odd, tile, row_first, row_second, col_first, col_second, stack):
    write_own(col_odd, tile, col_first, col_second, stack)
    far = stack.shape[0] - STEP
    write_ends(row_odd, row_first, row_second, stack.at[:STEP], stack.at[far:])


def forward_taps(weight):
    lines = [jnp.concatenate([weight[p, q] for q in range(3)], axis=1) for p in range(3)]
    return jnp.concatenate(lines, axis=0)


def backward_taps(weight):
    lines = [
        jnp.concatenate([weight[2 - p, 2 - q].T for q in range(3)], axis=1) for p in range(3)
    ]
    return jnp.concatenate(lines, axis=0)


def convolve(stack, weights, tile_rows, emit):
    channels = weights.shape[0] // 3
    cols = stack.shape[2]
    for pair in range(STEP // 2):
        products = []
        for k in range(tile_rows // STEP + 2):
            row = STEP * k + 2 * pair
            both = jnp.concatenate([stack[row], stack[row + 1]], axis=1)
            products.append(jnp.dot(weights, both, preferred_element_type=F32))
            if k >= 2:
                total = (
                    products[k - 2][:channels]
                    + products[k - 1][channels : 2 * channels]
                    + products[k][2 * channels :]
                )
                out_row = STEP * (k - 2) + 2 * pair
                emit(out_row, total[:, :cols])
                emit(out_row + 1, total[:, cols:])


def open_kernel(row_odd, col_odd, cot, x, tile, top, bottom, first, second, *rest):
    pieces, done = rest[:-1], rest[-1]
    group = pieces[0].shape[0]
    copies = [
        pltpu.make_async_copy(cot.at[pl.ds(j * group, group)], piece, done.at[j])
        for j, piece in enumerate(pieces)
    ]
    for copy in copies:
        copy.start()
    rows = x.shape[1]
    for a in range(0, rows, 16):
        tile[a : a + 16] = jnp.swapaxes(x[:, a : a + 16], 0, 1)
    write_edges(row_odd, col_odd, tile, top, bottom, first, second)
    for copy in copies:
        copy.wait()


def forward_kernel(row_odd, col_odd, tile, *refs):
    halo, (weight, bias, token, stack, slope, *pieces, kept) = refs[:4], refs[4:]
    token[...] = jnp.zeros_like(token)
    group = pieces[0].shape[0]
    tile_rows = tile.shape[0]
    write_shifted(row_odd, col_odd, tile, *halo, stack)
    channels = bias.shape[1]
    line = lax.broadcasted_iota(jnp.int32, (channels, channels), 0)
    lane = lax.broadcasted_iota(jnp.int32, (channels, channels), 1)
    offset = jnp.sum(jnp.where(line == lane, bias[...], 0.0), axis=1, keepdims=True)

    def emit(row, total):
        pre_act = total + offset
        rise = jnp.exp(jnp.minimum(pre_act, 0.0))
        slope[row] = rise
        elu = jnp.where(pre_act > 0, pre_act, rise - 1.0)
        kept[row] = (tile[row].astype(F32) + elu).astype(BF16)

    convolve(stack, forward_taps(weight), tile_rows, emit)
    for a in range(0, tile_rows, 16):
        mixed = jnp.swapaxes(kept[a : a + 16], 0, 1)
        for j, piece in enumerate(pieces):
            piece[:, a : a + 16] = mixed[j * group : (j + 1) * group]


def grad_pre_kernel(
    row_odd, col_odd, cot, keep, got, slope, token, tile, top, bottom, first, second, mirrored
):
    token[...] = jnp.zeros_like(token)
    rows = cot.shape[1]
    for a in range(0, rows, 16):
        turned = joined(row_odd[0], keep[:, a : a + 16], got[:, a : a + 16])
        mirrored[:, a : a + 16] = turned.astype(BF16)
        grad_mixed = cot[:, a : a + 16].astype(F32) + turned
        tile[a : a + 16] = (jnp.swapaxes(grad_mixed, 0, 1) * slope[a : a + 16]).astype(BF16)
    write_edges(row_odd, col_odd, tile, top, bottom, first, second)


def weight_kernel(side, row_odd, grad, stack, token, keep, give, packed):
    token[...] = jnp.zeros_like(token)
    tile_rows, channels, cols = grad.shape
    nothing = jnp.zeros((channels, cols), BF16)

    def taps(row):
        own = [row - STEP * p for p in range(3)]
        return jnp.concatenate([grad[a] if 0 <= a < tile_rows else nothing for a in own], axis=0)

    total = jnp.zeros((3 * channels, 3 * channels), F32)
    for row in range(0, tile_rows + 2 * STEP, 2):
        total = total + lax.dot_general(
            jnp.concatenate([taps(row), taps(row + 1)], axis=1),
            jnp.concatenate([stack[row], stack[row + 1]], axis=1),
            (((1,), (1,)), ((), ())),
            preferred_element_type=F32,
        )
    cells = jnp.zeros((channels, cols), F32)
    for row in range(tile_rows):
        cells = cells + grad[row].astype(F32)
    bias = jnp.broadcast_to(jnp.sum(cells, axis=1, keepdims=True), (channels, channels))
    blocks = [
        total[p * channels : (p + 1) * channels, q * channels : (q + 1) * channels]
        for p in range(3)
        for q in range(3)
    ] + [bias]
    for k in range(0, len(blocks), 2):
        at = k // 2 * channels
        packed[at : at + channels] = jnp.concatenate(blocks[k : k + 2], axis=1) * (1.0 / side)
    half = keep.shape[0]
    keep[...] = packed[pl.ds(row_odd[0] * half, half)]
    give[...] = packed[pl.ds((1 - row_odd[0]) * half, half)]


def unpack_kernel(row_odd, mine, other, weight, bias, packed):
    half, channels = mine.shape[0], weight.shape[2]
    packed[pl.ds(row_odd[0] * half, half)] = mine[...]
    packed[pl.ds((1 - row_odd[0]) * half, half)] = other[...]
    for k in range(9):
        row, col = k // 2 * channels, k % 2 * channels
        weight[k // 3, k % 3] = packed[row : row + channels, col : col + channels]
    last = packed[4 * channels :, channels:]
    line = lax.broadcasted_iota(jnp.int32, last.shape, 0)
    lane = lax.broadcasted_iota(jnp.int32, last.shape, 1)
    bias[...] = jnp.sum(jnp.where(line == lane, last, 0.0), axis=0, keepdims=True)


def input_grad_kernel(col_odd, tile, col_first, col_second, weight, cot, mirrored, *refs):
    token, out, ends, stack, kept = refs
    tile_rows = tile.shape[0]
    token[...] = jnp.zeros_like(token)
    for at in (0, tile_rows + STEP):
        stack[at : at + STEP] = jnp.zeros((STEP,) + stack.shape[1:], stack.dtype)
    write_own(col_odd, tile, col_first, col_second, stack)

    def emit(row, total):
        kept[row] = total

    convolve(stack, backward_taps(weight), tile_rows, emit)
    for a in range(0, tile_rows, 16):
        grad_mixed = cot[:, a : a + 16].astype(F32) + mirrored[:, a : a + 16].astype(F32)
        total = grad_mixed + jnp.swapaxes(kept[a : a + 16], 0, 1)
        if a == 0:
            ends[0] = total
        elif a == tile_rows - 16:
            ends[1] = total
        else:
            out[:, a : a + 16] = total.astype(BF16)


def input_grad_ends_kernel(row_odd, row_first, row_second, weight, ends, whole, out, *scratch):
    before, after, added, rounded, done = scratch
    channels, tile_rows = out.shape[:2]
    taps = backward_taps(weight)
    write_ends(row_odd, row_first, row_second, before, after)
    added[...] = jnp.zeros_like(added)
    for side, rows, tap, at in ((0, before, 0, 0), (1, after, 2, STEP)):
        own = taps[tap * channels : (tap + 1) * channels]
        for k in range(0, STEP, 2):
            both = jnp.concatenate([rows[k], rows[k + 1]], axis=1)
            total = jnp.dot(own, both, preferred_element_type=F32)
            cols = total.shape[1] // 2
            added[side, at + k] = total[:, :cols]
            added[side, at + k + 1] = total[:, cols:]
    copies = []
    for side, a in ((0, 0), (1, tile_rows - 16)):
        total = ends[side] + jnp.swapaxes(added[side], 0, 1)
        rounded[side] = total.astype(BF16)
        copy = pltpu.make_async_copy(
            rounded.at[side], out.at[:, pl.ds(a, 16)], done.at[side]
        )
        copy.start()
        copies.append(copy)
    for copy in copies:
        copy.wait()


def turn_kernel(unread, row_odd, *refs):
    pieces, (keep, give) = refs[unread:-2], refs[-2:]
    tile_rows = pieces[0].shape[1]
    core = row_odd[0]
    group, near = pieces[0].shape[0], len(pieces) // 2
    for j in range(near):
        for c in range(group):
            low, high = pieces[j][c].T, pieces[j + near][c].T
            first = jnp.concatenate([low[:tile_rows], high[:tile_rows]], axis=1)
            second = jnp.concatenate([low[tile_rows:], high[tile_rows:]], axis=1)
            keep[j * group + c] = jnp.where(core == 0, first, second)
            give[j * group + c] = jnp.where(core == 0, second, first)


def joined(core, keep, got):
    lower = lax.broadcasted_iota(jnp.int32, (1, 1, keep.shape[2]), 2) < keep.shape[2] // 2
    keep, got = keep.astype(F32), got.astype(F32)
    first, second = jnp.where(core == 0, keep, got), jnp.where(core == 0, got, keep)
    low = jnp.where(lower, first, pltpu.roll(second, keep.shape[2] // 2, 2))
    high = jnp.where(lower, pltpu.roll(first, keep.shape[2] // 2, 2), second)
    return jnp.concatenate([low, high], axis=0)


def detour(piece, far):
    if far == 0:
        return piece
    return lax.ppermute(piece, "row", [(r, r ^ (2 * far)) for r in range(lax.axis_size("row"))])


def cross(piece, far):
    size, blocks = lax.axis_size("row"), lax.axis_size("col")
    owners = [
        (r * blocks + z, (z * 2 + r % 2) * blocks + ((r // 2) ^ far))
        for r in range(size)
        for z in range(blocks)
    ]
    return lax.ppermute(piece, ("row", "col"), owners)


def turn(pieces, place, *after):
    group, tile_rows, tile_cols = pieces[0].shape
    half = shape((group * len(pieces) // 2, tile_rows, tile_cols), BF16)
    kernel = functools.partial(turn_kernel, len(after))
    return call(kernel, [half, half], place[0], *after, *pieces, name="turn")


def swapped(give):
    return lax.ppermute(give, "row", [(r, r ^ 1) for r in range(lax.axis_size("row"))])


def held(pieces, *until):
    return lax.optimization_barrier((pieces, until))[0]


def join_kernel(row_odd, keep, got, *refs):
    pieces, out = refs[:-1], refs[-1]
    for a in range(0, out.shape[1], 16):
        rows = slice(a, a + 16)
        turned = joined(row_odd[0], keep[:, rows], got[:, rows])
        own = jnp.concatenate([piece[:, rows] for piece in pieces], axis=0)
        out[:, rows] = (own.astype(F32) + turned).astype(BF16)


def summed(part, axis, reach):
    size = lax.axis_size(axis)
    while reach < size:
        part = part + lax.ppermute(part, axis, [(i, i ^ reach) for i in range(size)])
        reach *= 2
    return part


def shards(pair_feature_map, conv_weight, conv_bias, cotangent):
    channels, tile_rows, tile_cols = pair_feature_map.shape
    side = tile_rows * lax.axis_size("row")
    tile_shape = shape((tile_rows, channels, tile_cols), BF16)
    edges = edge_shapes(channels, tile_rows, tile_cols)
    stack_dims = (tile_rows + 2 * STEP, 3 * channels, tile_cols)
    conv_flops = 2 * 9 * channels * channels * tile_rows * tile_cols
    rounds = lax.axis_size("col")
    place = [jnp.full((1,), lax.axis_index(axis) % 2, jnp.int32) for axis in ("row", "col")]
    piece = shape((channels // rounds, tile_rows, tile_cols), BF16)

    tile, *opened = call(
        open_kernel,
        [tile_shape] + edges + [piece] * rounds,
        *place,
        cotangent,
        pair_feature_map,
        scratch=[pltpu.SemaphoreType.DMA((rounds,))],
        in_hbm=[2],
        out_hbm=rounds,
        name="open",
    )
    token = shape((8, 128), F32)
    dealt = [detour(p, j) for j, p in enumerate(opened[4:])]
    rows, strips = columns_of_halo(place, *opened[:4])
    halo = *rows_of_halo(rows), *strips
    forwarded, stack, slope, *mixed = call(
        forward_kernel,
        [token, shape(stack_dims, BF16), shape((tile_rows, channels, tile_cols), F32)]
        + [piece] * rounds,
        *place,
        tile,
        *halo,
        conv_weight,
        conv_bias[None],
        scratch=[pltpu.VMEM((tile_rows, channels, tile_cols), BF16)],
        flops=conv_flops,
        name="forward",
    )
    arrived = [cross(held(p, halo[2]), j) for j, p in enumerate(dealt)]
    mixed_dealt = [detour(p, j) for j, p in enumerate(mixed)]
    keep, give = turn(held(arrived, slope), place)
    ready, grad, *edge, mirrored = call(
        grad_pre_kernel,
        [token, tile_shape] + edges + [shape(cotangent.shape, BF16)],
        *place,
        cotangent,
        keep,
        swapped(give),
        slope,
        name="grad_pre",
    )
    packed = pltpu.VMEM((5 * channels, 2 * channels), F32)
    half = shape((5 * channels // 2, 2 * channels), F32)
    weighed, *terms = call(
        functools.partial(weight_kernel, side),
        [token, half, half],
        place[0],
        grad,
        stack,
        scratch=[packed],
        flops=conv_flops,
        name="weight_terms",
    )
    part = held(terms[0] + swapped(terms[1]), mixed_dealt[1])
    size = lax.axis_size("col")
    part = part + lax.ppermute(part, "col", [(i, i ^ 1) for i in range(size)])
    part = summed(held(part, mixed_dealt[2]), "col", 2)
    across = summed(part, "row", 2)
    rows, strips = columns_of_halo(place, *edge)
    mixed_arrived = [cross(held(p, part, *strips), j) for j, p in enumerate(mixed_dealt)]
    ended, grad_input, ends = call(
        input_grad_kernel,
        [token, shape(cotangent.shape, BF16), shape((2, channels, 16, tile_cols), F32)],
        place[1],
        grad,
        *strips,
        conv_weight,
        cotangent,
        mirrored,
        scratch=[
            pltpu.VMEM(stack_dims, BF16),
            pltpu.VMEM((tile_rows, channels, tile_cols), F32),
        ],
        flops=conv_flops,
        name="input_grad",
    )
    halo = rows_of_halo(rows)
    strip = pltpu.VMEM((STEP, 3 * channels, tile_cols), BF16)
    grad_input = call(
        input_grad_ends_kernel,
        shape(cotangent.shape, BF16),
        place[0],
        *halo,
        conv_weight,
        ends,
        grad_input,
        scratch=[
            strip,
            strip,
            pltpu.VMEM((2, 16, channels, tile_cols), F32),
            pltpu.VMEM((2, channels, 16, tile_cols), BF16),
            pltpu.SemaphoreType.DMA((2,)),
        ],
        in_hbm=[5],
        out_hbm=1,
        aliases={5: 0},
        name="input_grad_ends",
    )
    grad_weight, grad_bias = call(
        unpack_kernel,
        [shape((3, 3, channels, channels), F32), shape((1, channels), F32)],
        place[0],
        across,
        swapped(across),
        scratch=[packed],
        name="unpack",
    )
    mixed_keep, mixed_give = turn(held(mixed_arrived, across, *halo), place, ended)
    symmetric = call(
        join_kernel,
        shape(pair_feature_map.shape, BF16),
        place[0],
        mixed_keep,
        swapped(mixed_give),
        *mixed,
        name="join",
    )
    return symmetric, grad_input, grad_weight, grad_bias.reshape(channels)


def solution(mesh):
    placed = (P(None, "row", "col"), P(), P(), P(None, "row", "col"))
    return jax.shard_map(
        shards,
        mesh=mesh,
        in_specs=placed,
        out_specs=(P(None, "row", "col"), P(None, "row", "col"), P(), P()),
        check_vma=False,
    )
```

```python
import functools

import jax
import jax.numpy as jnp
from jax import lax
from jax.experimental import pallas as pl
from jax.experimental.pallas import tpu as pltpu
from jax.sharding import PartitionSpec as P

DILATION_STEP = 8
STEP = DILATION_STEP
BF16, F32 = jnp.bfloat16, jnp.float32
VMEM_LIMIT = 24 * 1024 * 1024


def call(
    kernel, out_shape, *args, scratch=(), flops=0, in_hbm=(), out_hbm=0, aliases=None, name=None
):
    in_specs = [
        pl.BlockSpec(memory_space=pltpu.SMEM if a.dtype == jnp.int32 else pltpu.VMEM) for a in args
    ]
    for k in in_hbm:
        in_specs[k] = pl.BlockSpec(memory_space=pl.ANY)
    out_specs = [pl.BlockSpec(memory_space=pltpu.VMEM)] * len(jax.tree.leaves(out_shape))
    if out_hbm:
        out_specs[-out_hbm:] = [pl.BlockSpec(memory_space=pl.ANY)] * out_hbm
    if not isinstance(out_shape, list):
        out_specs = out_specs[0]
    return pl.pallas_call(
        kernel,
        out_shape=out_shape,
        in_specs=in_specs,
        out_specs=out_specs,
        scratch_shapes=scratch,
        input_output_aliases=aliases or {},
        name=name,
        compiler_params=pltpu.CompilerParams(vmem_limit_bytes=VMEM_LIMIT),
        cost_estimate=pl.CostEstimate(
            flops=flops, bytes_accessed=0, transcendentals=0
        ),
    )(*args)


def shape(dims, dtype):
    return jax.ShapeDtypeStruct(tuple(dims), dtype)


def columns_of(rows, first):
    picked = [r[:, :STEP] if first else r[:, -STEP:] for r in rows]
    return jnp.concatenate(picked, axis=1)


def write_pair(parity, start, end, first, second):
    first[...] = jnp.where(parity == 0, end, start)
    second[...] = jnp.where(parity == 0, start, end)


def picked(parity, first, second):
    return jnp.where(parity == 0, second, first), jnp.where(parity == 0, first, second)


def write_edges(row_odd, col_odd, tile, top_ref, bottom_ref, first_ref, second_ref):
    tile_rows, _, tile_cols = tile.shape
    span = tile_cols // STEP
    for group in range(tile_rows // span):
        rows = [tile[group * span + k] for k in range(span)]
        write_pair(
            col_odd[0],
            columns_of(rows, True),
            columns_of(rows, False),
            first_ref.at[group],
            second_ref.at[group],
        )
    for k in range(STEP):
        top_ref[k] = tile[k]
        bottom_ref[k] = tile[tile_rows - STEP + k]


def edge_shapes(channels, tile_rows, tile_cols):
    rows = shape((STEP, channels, tile_cols), BF16)
    strips = shape((tile_rows * STEP // tile_cols, channels, tile_cols), BF16)
    return [rows, rows, strips, strips]


def exchanged(x, axis, turn):
    size = lax.axis_size(axis)
    pairs = [(i, i + 1) for i in range(turn, size - 1, 2)]
    return lax.ppermute(x, axis, pairs + [(j, i) for i, j in pairs])


def message_kernel(row_odd, col_odd, top, bottom, first, second, row_first, row_second):
    last = first.shape[0] - 1
    write_pair(row_odd[0], top[...], bottom[...], row_first.at[:STEP], row_second.at[:STEP])
    starts = picked(col_odd[0], first[0], second[0])
    ends = picked(col_odd[0], first[last], second[last])
    for k in range(2):
        write_pair(
            row_odd[0], starts[k], ends[k], row_first.at[STEP + k], row_second.at[STEP + k]
        )


def columns_of_halo(place, top, bottom, first, second):
    strips = exchanged(first, "col", 0), exchanged(second, "col", 1)
    message = shape((STEP + 2,) + top.shape[1:], BF16)
    rows = call(
        message_kernel, [message, message], *place, top, bottom, *strips, name="messages"
    )
    return rows, strips


def rows_of_halo(rows):
    near = exchanged(rows[0], "row", 0)
    return near, exchanged(held(rows[1], near), "row", 1)


def shifted(left, middle, right, lane, out):
    channels = middle.shape[0]
    left, right = left[:, lane : lane + STEP], right[:, lane : lane + STEP]
    out[:channels] = jnp.concatenate([left, middle[:, :-STEP]], axis=1)
    out[channels : 2 * channels] = middle
    out[2 * channels :] = jnp.concatenate([middle[:, STEP:], right], axis=1)


def write_own(col_odd, tile, col_first, col_second, stack):
    tile_rows, _, tile_cols = tile.shape
    span = tile_cols // STEP
    from_left, from_right = picked(col_odd[0], col_first[...], col_second[...])
    for row in range(tile_rows):
        group = row // span
        lane = STEP * (row % span)
        shifted(from_left[group], tile[row], from_right[group], lane, stack.at[STEP + row])


def write_ends(row_odd, row_first, row_second, before, after):
    span = row_first.shape[2] // STEP
    ends = picked(row_odd[0], row_first[...], row_second[...])
    for end, out, first in zip(ends, (before, after), (span - STEP, 0)):
        for k in range(STEP):
            shifted(end[STEP], end[k], end[STEP + 1], STEP * (first + k), out.at[k])


def write_shifted(row_odd, col_odd, tile, row_first, row_second, col_first, col_second, stack):
    write_own(col_odd, tile, col_first, col_second, stack)
    far = stack.shape[0] - STEP
    write_ends(row_odd, row_first, row_second, stack.at[:STEP], stack.at[far:])


def forward_taps(weight):
    lines = [jnp.concatenate([weight[p, q] for q in range(3)], axis=1) for p in range(3)]
    return jnp.concatenate(lines, axis=0)


def backward_taps(weight):
    lines = [
        jnp.concatenate([weight[2 - p, 2 - q].T for q in range(3)], axis=1) for p in range(3)
    ]
    return jnp.concatenate(lines, axis=0)


def convolve(stack, weights, tile_rows, emit):
    channels = weights.shape[0] // 3
    cols = stack.shape[2]
    for pair in range(STEP // 2):
        products = []
        for k in range(tile_rows // STEP + 2):
            row = STEP * k + 2 * pair
            both = jnp.concatenate([stack[row], stack[row + 1]], axis=1)
            products.append(jnp.dot(weights, both, preferred_element_type=F32))
            if k >= 2:
                total = (
                    products[k - 2][:channels]
                    + products[k - 1][channels : 2 * channels]
                    + products[k][2 * channels :]
                )
                out_row = STEP * (k - 2) + 2 * pair
                emit(out_row, total[:, :cols])
                emit(out_row + 1, total[:, cols:])


def open_kernel(row_odd, col_odd, cot, x, tile, top, bottom, first, second, *rest):
    pieces, done = rest[:-1], rest[-1]
    group = pieces[0].shape[0]
    copies = [
        pltpu.make_async_copy(cot.at[pl.ds(j * group, group)], piece, done.at[j])
        for j, piece in enumerate(pieces)
    ]
    for copy in copies:
        copy.start()
    rows = x.shape[1]
    for a in range(0, rows, 16):
        tile[a : a + 16] = jnp.swapaxes(x[:, a : a + 16], 0, 1)
    write_edges(row_odd, col_odd, tile, top, bottom, first, second)
    for copy in copies:
        copy.wait()


def forward_kernel(row_odd, col_odd, tile, *refs):
    halo, (weight, bias, token, stack, slope, *pieces, kept) = refs[:4], refs[4:]
    token[...] = jnp.zeros_like(token)
    group = pieces[0].shape[0]
    tile_rows = tile.shape[0]
    write_shifted(row_odd, col_odd, tile, *halo, stack)
    offset = bias[...]

    def emit(row, total):
        pre_act = total + offset
        rise = jnp.exp(jnp.minimum(pre_act, 0.0))
        slope[row] = rise
        elu = jnp.where(pre_act > 0, pre_act, rise - 1.0)
        kept[row] = (tile[row].astype(F32) + elu).astype(BF16)

    convolve(stack, forward_taps(weight), tile_rows, emit)
    for a in range(0, tile_rows, 16):
        mixed = jnp.swapaxes(kept[a : a + 16], 0, 1)
        for j, piece in enumerate(pieces):
            piece[:, a : a + 16] = mixed[j * group : (j + 1) * group]


def grad_pre_kernel(
    row_odd, col_odd, cot, keep, got, slope, token, tile, top, bottom, first, second, mirrored
):
    token[...] = jnp.zeros_like(token)
    rows = cot.shape[1]
    for a in range(0, rows, 16):
        turned = joined(row_odd[0], keep[:, a : a + 16], got[:, a : a + 16])
        mirrored[:, a : a + 16] = turned.astype(BF16)
        grad_mixed = cot[:, a : a + 16].astype(F32) + turned
        tile[a : a + 16] = (jnp.swapaxes(grad_mixed, 0, 1) * slope[a : a + 16]).astype(BF16)
    write_edges(row_odd, col_odd, tile, top, bottom, first, second)


def weight_kernel(side, row_odd, grad, stack, token, keep, give, packed):
    token[...] = jnp.zeros_like(token)
    tile_rows, channels, cols = grad.shape
    nothing = jnp.zeros((channels, cols), BF16)

    def taps(row):
        own = [row - STEP * p for p in range(3)]
        return jnp.concatenate([grad[a] if 0 <= a < tile_rows else nothing for a in own], axis=0)

    total = jnp.zeros((3 * channels, 3 * channels), F32)
    for row in range(0, tile_rows + 2 * STEP, 2):
        total = total + lax.dot_general(
            jnp.concatenate([taps(row), taps(row + 1)], axis=1),
            jnp.concatenate([stack[row], stack[row + 1]], axis=1),
            (((1,), (1,)), ((), ())),
            preferred_element_type=F32,
        )
    cells = jnp.zeros((channels, cols), F32)
    for row in range(tile_rows):
        cells = cells + grad[row].astype(F32)
    bias = jnp.broadcast_to(jnp.sum(cells, axis=1, keepdims=True), (channels, channels))
    blocks = [
        total[p * channels : (p + 1) * channels, q * channels : (q + 1) * channels]
        for p in range(3)
        for q in range(3)
    ] + [bias]
    for k in range(0, len(blocks), 2):
        at = k // 2 * channels
        packed[at : at + channels] = jnp.concatenate(blocks[k : k + 2], axis=1) * (1.0 / side)
    half = keep.shape[0]
    keep[...] = packed[pl.ds(row_odd[0] * half, half)]
    give[...] = packed[pl.ds((1 - row_odd[0]) * half, half)]


def unpack_kernel(row_odd, mine, other, weight, bias, packed):
    half, channels = mine.shape[0], weight.shape[2]
    packed[pl.ds(row_odd[0] * half, half)] = mine[...]
    packed[pl.ds((1 - row_odd[0]) * half, half)] = other[...]
    for k in range(9):
        row, col = k // 2 * channels, k % 2 * channels
        weight[k // 3, k % 3] = packed[row : row + channels, col : col + channels]
    last = packed[4 * channels :, channels:]
    line = lax.broadcasted_iota(jnp.int32, last.shape, 0)
    lane = lax.broadcasted_iota(jnp.int32, last.shape, 1)
    bias[...] = jnp.sum(jnp.where(line == lane, last, 0.0), axis=0, keepdims=True)


def input_grad_kernel(col_odd, tile, col_first, col_second, weight, cot, mirrored, *refs):
    token, out, ends, stack, kept = refs
    tile_rows = tile.shape[0]
    token[...] = jnp.zeros_like(token)
    for at in (0, tile_rows + STEP):
        stack[at : at + STEP] = jnp.zeros((STEP,) + stack.shape[1:], stack.dtype)
    write_own(col_odd, tile, col_first, col_second, stack)

    def emit(row, total):
        kept[row] = total

    convolve(stack, backward_taps(weight), tile_rows, emit)
    for a in range(0, tile_rows, 16):
        grad_mixed = cot[:, a : a + 16].astype(F32) + mirrored[:, a : a + 16].astype(F32)
        total = grad_mixed + jnp.swapaxes(kept[a : a + 16], 0, 1)
        if a == 0:
            ends[0] = total
        elif a == tile_rows - 16:
            ends[1] = total
        else:
            out[:, a : a + 16] = total.astype(BF16)


def input_grad_ends_kernel(row_odd, row_first, row_second, weight, ends, whole, out, *scratch):
    before, after, added, rounded, done = scratch
    channels, tile_rows = out.shape[:2]
    taps = backward_taps(weight)
    write_ends(row_odd, row_first, row_second, before, after)
    added[...] = jnp.zeros_like(added)
    for side, rows, tap, at in ((0, before, 0, 0), (1, after, 2, STEP)):
        own = taps[tap * channels : (tap + 1) * channels]
        for k in range(0, STEP, 2):
            both = jnp.concatenate([rows[k], rows[k + 1]], axis=1)
            total = jnp.dot(own, both, preferred_element_type=F32)
            cols = total.shape[1] // 2
            added[side, at + k] = total[:, :cols]
            added[side, at + k + 1] = total[:, cols:]
    copies = []
    for side, a in ((0, 0), (1, tile_rows - 16)):
        total = ends[side] + jnp.swapaxes(added[side], 0, 1)
        rounded[side] = total.astype(BF16)
        copy = pltpu.make_async_copy(
            rounded.at[side], out.at[:, pl.ds(a, 16)], done.at[side]
        )
        copy.start()
        copies.append(copy)
    for copy in copies:
        copy.wait()


def turn_kernel(unread, row_odd, *refs):
    pieces, (keep, give) = refs[unread:-2], refs[-2:]
    tile_rows = pieces[0].shape[1]
    core = row_odd[0]
    group, near = pieces[0].shape[0], len(pieces) // 2
    for j in range(near):
        for c in range(group):
            low, high = pieces[j][c].T, pieces[j + near][c].T
            first = jnp.concatenate([low[:tile_rows], high[:tile_rows]], axis=1)
            second = jnp.concatenate([low[tile_rows:], high[tile_rows:]], axis=1)
            keep[j * group + c] = jnp.where(core == 0, first, second)
            give[j * group + c] = jnp.where(core == 0, second, first)


def joined(core, keep, got):
    lower = lax.broadcasted_iota(jnp.int32, (1, 1, keep.shape[2]), 2) < keep.shape[2] // 2
    keep, got = keep.astype(F32), got.astype(F32)
    first, second = jnp.where(core == 0, keep, got), jnp.where(core == 0, got, keep)
    low = jnp.where(lower, first, pltpu.roll(second, keep.shape[2] // 2, 2))
    high = jnp.where(lower, pltpu.roll(first, keep.shape[2] // 2, 2), second)
    return jnp.concatenate([low, high], axis=0)


def detour(piece, far):
    if far == 0:
        return piece
    return lax.ppermute(piece, "row", [(r, r ^ (2 * far)) for r in range(lax.axis_size("row"))])


def cross(piece, far):
    size, blocks = lax.axis_size("row"), lax.axis_size("col")
    owners = [
        (r * blocks + z, (z * 2 + r % 2) * blocks + ((r // 2) ^ far))
        for r in range(size)
        for z in range(blocks)
    ]
    return lax.ppermute(piece, ("row", "col"), owners)


def turn(pieces, place, *after):
    group, tile_rows, tile_cols = pieces[0].shape
    half = shape((group * len(pieces) // 2, tile_rows, tile_cols), BF16)
    kernel = functools.partial(turn_kernel, len(after))
    return call(kernel, [half, half], place[0], *after, *pieces, name="turn")


def swapped(give):
    return lax.ppermute(give, "row", [(r, r ^ 1) for r in range(lax.axis_size("row"))])


def held(pieces, *until):
    return lax.optimization_barrier((pieces, until))[0]


def join_kernel(row_odd, keep, got, *refs):
    pieces, out = refs[:-1], refs[-1]
    for a in range(0, out.shape[1], 16):
        rows = slice(a, a + 16)
        turned = joined(row_odd[0], keep[:, rows], got[:, rows])
        own = jnp.concatenate([piece[:, rows] for piece in pieces], axis=0)
        out[:, rows] = (own.astype(F32) + turned).astype(BF16)


def summed(part, axis, reach):
    size = lax.axis_size(axis)
    while reach < size:
        part = part + lax.ppermute(part, axis, [(i, i ^ reach) for i in range(size)])
        reach *= 2
    return part


def shards(pair_feature_map, conv_weight, conv_bias, cotangent):
    channels, tile_rows, tile_cols = pair_feature_map.shape
    side = tile_rows * lax.axis_size("row")
    tile_shape = shape((tile_rows, channels, tile_cols), BF16)
    edges = edge_shapes(channels, tile_rows, tile_cols)
    stack_dims = (tile_rows + 2 * STEP, 3 * channels, tile_cols)
    conv_flops = 2 * 9 * channels * channels * tile_rows * tile_cols
    rounds = lax.axis_size("col")
    place = [jnp.full((1,), lax.axis_index(axis) % 2, jnp.int32) for axis in ("row", "col")]
    piece = shape((channels // rounds, tile_rows, tile_cols), BF16)

    tile, *opened = call(
        open_kernel,
        [tile_shape] + edges + [piece] * rounds,
        *place,
        cotangent,
        pair_feature_map,
        scratch=[pltpu.SemaphoreType.DMA((rounds,))],
        in_hbm=[2],
        out_hbm=rounds,
        name="open",
    )
    token = shape((8, 128), F32)
    dealt = [detour(p, j) for j, p in enumerate(opened[4:])]
    rows, strips = columns_of_halo(place, *opened[:4])
    halo = *rows_of_halo(rows), *strips
    forwarded, stack, slope, *mixed = call(
        forward_kernel,
        [token, shape(stack_dims, BF16), shape((tile_rows, channels, tile_cols), F32)]
        + [piece] * rounds,
        *place,
        tile,
        *halo,
        conv_weight,
        conv_bias[:, None],
        scratch=[pltpu.VMEM((tile_rows, channels, tile_cols), BF16)],
        flops=conv_flops,
        name="forward",
    )
    arrived = [cross(held(p, halo[2]), j) for j, p in enumerate(dealt)]
    mixed_dealt = [detour(p, j) for j, p in enumerate(mixed)]
    keep, give = turn(held(arrived, slope), place)
    ready, grad, *edge, mirrored = call(
        grad_pre_kernel,
        [token, tile_shape] + edges + [shape(cotangent.shape, BF16)],
        *place,
        cotangent,
        keep,
        swapped(give),
        slope,
        name="grad_pre",
    )
    packed = pltpu.VMEM((5 * channels, 2 * channels), F32)
    half = shape((5 * channels // 2, 2 * channels), F32)
    weighed, *terms = call(
        functools.partial(weight_kernel, side),
        [token, half, half],
        place[0],
        grad,
        stack,
        scratch=[packed],
        flops=conv_flops,
        name="weight_terms",
    )
    part = held(terms[0] + swapped(terms[1]), mixed_dealt[1])
    size = lax.axis_size("col")
    part = part + lax.ppermute(part, "col", [(i, i ^ 1) for i in range(size)])
    part = summed(held(part, mixed_dealt[2]), "col", 2)
    across = summed(part, "row", 2)
    rows, strips = columns_of_halo(place, *edge)
    mixed_arrived = [cross(held(p, part, *strips), j) for j, p in enumerate(mixed_dealt)]
    ended, grad_input, ends = call(
        input_grad_kernel,
        [token, shape(cotangent.shape, BF16), shape((2, channels, 16, tile_cols), F32)],
        place[1],
        grad,
        *strips,
        conv_weight,
        cotangent,
        mirrored,
        scratch=[
            pltpu.VMEM(stack_dims, BF16),
            pltpu.VMEM((tile_rows, channels, tile_cols), F32),
        ],
        flops=conv_flops,
        name="input_grad",
    )
    halo = rows_of_halo(rows)
    strip = pltpu.VMEM((STEP, 3 * channels, tile_cols), BF16)
    grad_input = call(
        input_grad_ends_kernel,
        shape(cotangent.shape, BF16),
        place[0],
        *halo,
        conv_weight,
        ends,
        grad_input,
        scratch=[
            strip,
            strip,
            pltpu.VMEM((2, 16, channels, tile_cols), F32),
            pltpu.VMEM((2, channels, 16, tile_cols), BF16),
            pltpu.SemaphoreType.DMA((2,)),
        ],
        in_hbm=[5],
        out_hbm=1,
        aliases={5: 0},
        name="input_grad_ends",
    )
    grad_weight, grad_bias = call(
        unpack_kernel,
        [shape((3, 3, channels, channels), F32), shape((1, channels), F32)],
        place[0],
        across,
        swapped(across),
        scratch=[packed],
        name="unpack",
    )
    mixed_keep, mixed_give = turn(held(mixed_arrived, across, *halo), place, ended)
    symmetric = call(
        join_kernel,
        shape(pair_feature_map.shape, BF16),
        place[0],
        mixed_keep,
        swapped(mixed_give),
        *mixed,
        name="join",
    )
    return symmetric, grad_input, grad_weight, grad_bias.reshape(channels)


def solution(mesh):
    placed = (P(None, "row", "col"), P(), P(), P(None, "row", "col"))
    return jax.shard_map(
        shards,
        mesh=mesh,
        in_specs=placed,
        out_specs=(P(None, "row", "col"), P(None, "row", "col"), P(), P()),
        check_vma=False,
    )
```
